512 devices in a mesh: slab: 64 (over z, y_lo, core), grp: 8 (over y_hi, x).
Axes of the slice: x: 4, y: 8 (y_hi: 2, y_lo: 4; y = y_hi * 4 + y_lo), z: 8, core: 2. Of those that a mesh axis runs over, the one named last changes fastest.
Arguments:
- sound_speed: float32 [64, 256, 256], P('slab'), may hold values from 0.5 to 1
- density: float32 [64, 256, 256], P('slab'), may hold values from 0.7 to 1.4
- attenuation: float32 [64, 256, 256], P('slab'), may hold values from 0.01 to 0.2
- wavelet: float32 [4], replicated, may hold values from -4 to 4
- weights: bfloat16 [8, 1024], replicated, may hold values from -4 to 4
- emitter_group: int32 [1024], replicated, may hold values from 0 to 7
- emitter_cell: int32 [1024], replicated, may hold values from 0 to 4194303, as said below
- receiver_cell: int32 [8192], P('slab'), may hold values from 0 to 65535, as said below
- pressure_start: float32 [8, 64, 256, 256], P('grp', 'slab'), may hold values from -6 to 6
- velocity_start: float32 [3, 8, 64, 256, 256], P(None, 'grp', 'slab'), may hold values from -3 to 3
- observed: bfloat16 [1024, 4, 8192], P('grp', None, 'slab'), may hold values from -0.59765625 to 0.59765625
Outputs:
- grad_speed: float32 [64, 256, 256], P('slab', 'grp')
- grad_atten: float32 [64, 256, 256], P('slab', 'grp')
The draws below stay inside these ranges and needn't reach their ends.
Inputs may be any that keep to these rules, and one draw needn't show every extreme that they name: `emitter_cell`: each emitter sits at the cell of some receiver (the transducers both emit and record); several emitters may share a cell. `receiver_cell`: cells are counted within the 1 x 256 x 256 block of the receiver's own slab, z slowest and y fastest; several receivers may share a cell. `emitter_group`: the group of encoded sources that an emitter takes part in.
All inputs are finite; a program needn't handle non-finite values.
Results may differ from the reference program's by a relative error of at most 0.0003.
Values may be sent and summed in bfloat16 or wider, within the bound.
A program may use at most 64 MiB of HBM per device.

```python
import math
import jax
import jax.numpy as jnp
from jax import lax

Z_DEV = 1
NX = 256
NY = 256
NT = 4
S_DEV = 1
REC_DEV = 128
NZ = 64
SHOTS = 8
EMIT = 1024
NREC = 8192
N_GRP = 8


def transducer_cells(key):
    receiver_local = jax.random.randint(jax.random.fold_in(key, 711), (NREC,), 0, Z_DEV * NX * NY).astype(jnp.int32)
    chosen = jax.random.randint(jax.random.fold_in(key, 712), (EMIT,), 0, NREC).astype(jnp.int32)
    emitter_global = receiver_local[chosen] + chosen // REC_DEV * (Z_DEV * NX * NY)
    return (receiver_local, emitter_global.astype(jnp.int32))


def draw_receiver_cell(key, part):
    return transducer_cells(key)[0]


def draw_emitter_cell(key, part):
    return transducer_cells(key)[1]


def plant(values, rng, low, largest):
    spot = [jax.random.randint(jax.random.fold_in(rng, axis), (), 0, length) for axis, length in enumerate(values.shape)]
    widest = values.shape.index(max(values.shape))
    beside = spot[:widest] + [(spot[widest] + 1) % values.shape[widest]] + spot[widest + 1:]
    return values.at[tuple(spot)].set(low).at[tuple(beside)].set(largest)


def steps_of(stream_key, shape, pieces, smallest, top_value):
    def one(axis_at, parts):
        steps = jax.random.uniform(jax.random.fold_in(jax.random.fold_in(stream_key, 6), axis_at), (parts,), jnp.float32, smallest / len(pieces), top_value / len(pieces))
        return jnp.repeat(jnp.exp(steps), shape[axis_at] // parts).reshape((-1,) + (1,) * (len(shape) - axis_at - 1))

    level = one(*pieces[0])
    for cut in pieces[1:]:
        level = level * one(*cut)
    return level


def normal_values(key, shape, spread, most, shards=(), dtype=jnp.bfloat16):
    array = spread * jax.random.normal(key, shape, jnp.float32)
    if shards:
        array = array * steps_of(key, shape, shards, -0.22, 0.18)
    return jnp.clip(array, -most, most).astype(dtype)


def setup_inputs(seed: int = 0) -> dict:
    seeds = jax.random.split(jax.random.key(seed), 12)
    sound_speed = jnp.clip(0.5 + 0.5 * jax.random.uniform(seeds[0], (NZ, NX, NY), jnp.float32) ** steps_of(seeds[0], (NZ, NX, NY), ((0, 64),), -0.2, 0.2), 0.5, 1.0)
    density = jnp.clip(0.7 + 0.7 * jax.random.uniform(seeds[1], (NZ, NX, NY), jnp.float32) ** steps_of(seeds[1], (NZ, NX, NY), ((0, 64),), -0.2, 0.2), 0.7, 1.4)
    attenuation = jnp.clip(jnp.exp(math.log(0.2) - 2.9957323 * jax.random.uniform(seeds[2], (NZ, NX, NY), jnp.float32) ** steps_of(seeds[2], (NZ, NX, NY), ((0, 64),), -0.2, 0.2)), 0.01, 0.2)
    wavelet = normal_values(seeds[3], (NT,), 1.0, 4.0, (), jnp.float32)
    weights = normal_values(seeds[4], (SHOTS, EMIT), 1.0, 4.0)
    emitter_group = plant(jax.random.randint(seeds[5], (EMIT,), 0, N_GRP), jax.random.fold_in(seeds[5], 1), 0, N_GRP - 1).astype(jnp.int32)
    emitter_cell = draw_emitter_cell(jax.random.fold_in(seeds[11], 71), 0)
    receiver_cell = draw_receiver_cell(jax.random.fold_in(seeds[11], 71), 0)
    pressure_start = normal_values(seeds[8], (SHOTS, NZ, NX, NY), 1.0, 6.0, ((0, 8), (1, 64)), jnp.float32)
    velocity_start = normal_values(seeds[9], (3, SHOTS, NZ, NX, NY), 0.5, 3.0, ((1, 8), (2, 64)), jnp.float32)
    observed = normal_values(seeds[10], (EMIT, NT, NREC), 0.1, 0.59765625, ((0, 8), (2, 64)))
    return dict(sound_speed=sound_speed, density=density, attenuation=attenuation, wavelet=wavelet, weights=weights, emitter_group=emitter_group, emitter_cell=emitter_cell, receiver_cell=receiver_cell, pressure_start=pressure_start, velocity_start=velocity_start, observed=observed)


step_ratio = 0.5

def up_diff(grid_field, along_dim):
    extent = grid_field.shape[along_dim]
    zero_plane = jnp.zeros_like(lax.slice_in_dim(grid_field, 0, 1, axis=along_dim))
    shifted = jnp.concatenate([lax.slice_in_dim(grid_field, 1, extent, axis=along_dim), zero_plane], axis=along_dim)
    return shifted - grid_field

def down_diff(grid_field, along_dim):
    extent = grid_field.shape[along_dim]
    zero_plane = jnp.zeros_like(lax.slice_in_dim(grid_field, 0, 1, axis=along_dim))
    behind = jnp.concatenate([zero_plane, lax.slice_in_dim(grid_field, 0, extent - 1, axis=along_dim)], axis=along_dim)
    return grid_field - behind

def shot_misfit(sound_speed, attenuation, density, amplitude, pressure, velocity, wavelet, encoded, receiver_global, shots_total):
    kappa_field = density * sound_speed * sound_speed
    buoyancy = 1.0 / density
    keep_rate = 1.0 - attenuation
    moving = [velocity[0], velocity[1], velocity[2]]
    recorded = []
    for step_index in range(NT):
        moving = [moving[dim_index] - step_ratio * buoyancy * up_diff(pressure, dim_index) for dim_index in range(3)]
        div_field = down_diff(moving[0], 0) + down_diff(moving[1], 1) + down_diff(moving[2], 2)
        pressure = keep_rate * pressure - step_ratio * kappa_field * div_field + wavelet[step_index] * amplitude
        recorded.append(pressure.reshape(-1)[receiver_global])
    residual = jnp.stack(recorded) - encoded
    return jnp.sum(residual * residual) / (2.0 * shots_total)

def reference(sound_speed, density, attenuation, wavelet, weights, emitter_group, emitter_cell, receiver_cell, pressure_start, velocity_start, observed):
    shots_total = weights.shape[0]
    owner_group = (jnp.arange(shots_total) // S_DEV).astype(jnp.int32)
    active = jnp.where(emitter_group[None, :] == owner_group[:, None], weights, jnp.zeros_like(weights))
    slab_offset = (jnp.arange(NREC) // REC_DEV).astype(jnp.int32) * (Z_DEV * NX * NY)
    receiver_global = receiver_cell.astype(jnp.int32) + slab_offset
    flat_obs = observed.reshape(EMIT, NT * NREC)

    def per_shot(running, shot_index):
        shot_weights = active[shot_index]
        encoded = jnp.dot(shot_weights[None, :], flat_obs, preferred_element_type=jnp.float32).reshape(NT, NREC)
        amplitude = jnp.zeros((NZ * NX * NY,), jnp.float32).at[emitter_cell].add(shot_weights.astype(jnp.float32)).reshape(NZ, NX, NY)
        shot_grads = jax.grad(shot_misfit, argnums=(0, 1))(sound_speed, attenuation, density, amplitude, pressure_start[shot_index], velocity_start[:, shot_index], wavelet, encoded, receiver_global, shots_total)
        return ((running[0] + shot_grads[0], running[1] + shot_grads[1]), None)
    initial = (jnp.zeros_like(sound_speed), jnp.zeros_like(attenuation))
    totals, unused = lax.scan(per_shot, initial, jnp.arange(shots_total))
    return (totals[0], totals[1])
```

```python
import functools
import jax
import jax.numpy as jnp
from jax import lax
from jax.experimental import pallas as pl
from jax.experimental.pallas import tpu as pltpu
from jax.sharding import PartitionSpec as P

MESH = pl.DeviceIdType.MESH
HALF = 0.5
F32 = jnp.float32
BF16 = jnp.bfloat16


def split3(v):
    hi = v.astype(BF16)
    rest = v - hi.astype(F32)
    mid = rest.astype(BF16)
    low = (rest - mid.astype(F32)).astype(BF16)
    return hi, mid, low


def kernel(
    n_slab, n_grp,
    wav, speed_h, dens_h, atten_h, press_h, vel_h, weights, group, ecell, rcell, obs,
    out_s, out_a,
    speed, dens, atten, press, vel, wup, bup, pdn, wlow, blow,
    pabove, pbelow, sabove, sbelow, scaled, encsend, encrecv, grad, gradrecv,
    load_sem, halo_send, halo_recv, enc_send, enc_recv, grad_send, grad_recv,
):
    steps = 4
    slab = lax.axis_index("slab")
    grp = lax.axis_index("grp")
    above = lax.rem(slab + 1, n_slab)
    below = lax.rem(slab + n_slab - 1, n_slab)

    loads = [
        pltpu.make_async_copy(src, dst, load_sem.at[i])
        for i, (src, dst) in enumerate([
            (press_h.at[0, 0], press.at[0]), (dens_h.at[0], dens), (vel_h.at[:, 0, 0], vel),
            (speed_h.at[0], speed), (atten_h.at[0], atten),
        ])
    ]
    for c in loads:
        c.start()

    barrier = pltpu.get_barrier_semaphore()
    for s in (above, below):
        pl.semaphore_signal(barrier, inc=1, device_id=(s, grp), device_id_type=MESH)
    for d in range(1, n_grp):
        pl.semaphore_signal(
            barrier, inc=1, device_id=(slab, lax.rem(grp + d, n_grp)), device_id_type=MESH)
    pl.semaphore_wait(barrier, n_grp + 1)

    def send(src, dst, to, k):
        c = pltpu.make_async_remote_copy(
            src_ref=src, dst_ref=dst, send_sem=halo_send.at[k], recv_sem=halo_recv.at[k],
            device_id=(to, grp), device_id_type=MESH)
        c.start()
        return c

    pending = []
    for c in loads[:3]:
        c.wait()
    p0_down = send(press.at[0], pdn, below, 0)
    buoy = 1.0 / dens[...]
    bup[...] = buoy
    wup[...] = vel[0] + HALF * buoy * press[0]
    w_up = send(wup, wlow, above, 1)
    b_up = send(bup, blow, above, 2)

    wall = weights[...].astype(F32)
    shot_row = lax.broadcasted_iota(jnp.int32, wall.shape, 0)
    active = jnp.where(group[...] == shot_row, wall, 0.0)
    own = jnp.sum(jnp.where(shot_row == grp, active, 0.0), axis=0, keepdims=True)
    emit = wall.shape[1]
    ec = ecell[...] - slab * 65536
    inside = (ec >= 0) & (ec < 65536)
    ex = jnp.where(inside, ec >> 8, -1)
    ey = ec & 255
    row_e = lax.broadcasted_iota(jnp.int32, (256, emit), 0)
    ax = jnp.where(row_e == ex, own, 0.0).astype(BF16)
    ay = jnp.where(row_e == ey, 1.0, 0.0).astype(BF16)
    nt = (((1,), (1,)), ((), ()))
    amp = lax.dot_general(ax, ay, nt, preferred_element_type=F32)

    e_dev = obs.shape[0]
    eoff = pl.multiple_of(grp * e_dev, 128)
    wdev = weights[:, pl.ds(eoff, e_dev)].astype(F32)
    gdev = group[:, pl.ds(eoff, e_dev)]
    act_dev = jnp.where(
        gdev == lax.broadcasted_iota(jnp.int32, wdev.shape, 0), wdev, 0.0).astype(BF16)
    er = lax.broadcasted_iota(jnp.int32, (e_dev, e_dev * steps), 0)
    el = lax.broadcasted_iota(jnp.int32, (e_dev, e_dev * steps), 1)
    expand = jnp.where((el >> 2) == er, 1.0, 0.0).astype(BF16)
    wide = jnp.dot(act_dev, expand, preferred_element_type=F32).astype(BF16)
    rr = lax.broadcasted_iota(jnp.int32, (8 * n_grp, n_grp), 0)
    rl = lax.broadcasted_iota(jnp.int32, (8 * n_grp, n_grp), 1)
    rows = jnp.where((rr >> 3) == rl, 1.0, 0.0).astype(BF16)
    tall = jnp.dot(rows, wide, preferred_element_type=F32)
    tr = lax.broadcasted_iota(jnp.int32, tall.shape, 0)
    tl = lax.broadcasted_iota(jnp.int32, tall.shape, 1)
    lhs = jnp.where((tr & 7) == (tl & 3), tall, 0.0).astype(BF16)
    flat = obs[...].astype(F32).reshape(e_dev * steps, obs.shape[2]).astype(BF16)
    part = jnp.dot(lhs, flat, preferred_element_type=F32)
    encsend[...] = part.reshape(encsend.shape)
    for d in range(1, n_grp):
        peer = lax.rem(grp + d, n_grp)
        c = pltpu.make_async_remote_copy(
            src_ref=encsend.at[peer], dst_ref=encrecv.at[d], send_sem=enc_send.at[d],
            recv_sem=enc_recv.at[d], device_id=(slab, peer), device_id_type=MESH)
        c.start()
        pending.append(c)
    enc_copies = list(pending)

    rc = rcell[...]
    row_r = lax.broadcasted_iota(jnp.int32, (256, rc.shape[1]), 0)
    rx = jnp.where(row_r == (rc >> 8), 1.0, 0.0)
    ry = jnp.where(row_r == (rc & 255), 1.0, 0.0).astype(BF16)
    ry3 = jnp.concatenate([ry, ry, ry], axis=1)

    def record(field):
        total = 0.0
        for piece in split3(field):
            total = total + jnp.dot(piece, ry, preferred_element_type=F32)
        return jnp.sum(total * rx, axis=0, keepdims=True)

    def inject(values):
        pieces = [(rx * v.astype(F32)).astype(BF16) for v in split3(values)]
        return lax.dot_general(
            jnp.concatenate(pieces, axis=1), ry3, nt, preferred_element_type=F32)

    xi = lax.broadcasted_iota(jnp.int32, (256, 256), 0)
    yi = lax.broadcasted_iota(jnp.int32, (256, 256), 1)

    def up_x(f):
        return jnp.where(xi == 255, 0.0, pltpu.roll(f, 255, 0)) - f

    def up_y(f):
        return jnp.where(yi == 255, 0.0, pltpu.roll(f, 255, 1)) - f

    def down_x(f):
        return f - jnp.where(xi == 0, 0.0, pltpu.roll(f, 1, 0))

    def down_y(f):
        return f - jnp.where(yi == 0, 0.0, pltpu.roll(f, 1, 1))

    has_above = slab < n_slab - 1
    has_below = slab > 0
    for c in loads[3:]:
        c.wait()
    kappa = dens[...] * speed[...] * speed[...]
    keep = 1.0 - atten[...]

    divs = []
    recorded = []
    pz, px, py = vel[0], vel[1], vel[2]
    p = press[0]
    p0_down.wait_recv()
    w_up.wait_recv()
    b_up.wait_recv()
    b_low = jnp.where(has_below, blow[...], 0.0)
    for t in range(steps):
        if t == 0:
            pa = jnp.where(has_above, pdn[...], 0.0)
            pzl = jnp.where(has_below, wlow[...], 0.0) - HALF * b_low * p
        else:
            dn = send(press.at[t], pabove.at[t - 1], below, 3 + 2 * (t - 1))
            up = send(press.at[t], pbelow.at[t - 1], above, 4 + 2 * (t - 1))
            dn.wait_recv()
            up.wait_recv()
            pending += [dn, up]
            pa = jnp.where(has_above, pabove[t - 1], 0.0)
            pzl = pzl - HALF * b_low * (p - pbelow[t - 1])
        pz = pz - HALF * buoy * (pa - p)
        px = px - HALF * buoy * up_x(p)
        py = py - HALF * buoy * up_y(p)
        div = pz - pzl + down_x(px) + down_y(py)
        divs.append(div)
        p = keep * p - HALF * kappa * div + wav[t] * amp
        if t < steps - 1:
            press[t + 1] = p
        recorded.append(record(p))

    for c in enc_copies:
        c.wait_recv()
    enc = encsend[grp]
    for d in range(1, n_grp):
        enc = enc + encrecv[d]

    lp = jnp.zeros((256, 256), F32)
    lz = lx = ly = lzl = lp
    gk = gd = lp
    for t in reversed(range(steps)):
        residual = (recorded[t] - enc[t:t + 1]) * (1.0 / n_grp)
        adj = lp + inject(residual)
        gd = gd - adj * press[t]
        gk = gk - HALF * adj * divs[t]
        if t > 0:
            s = kappa * adj
            scaled[t - 1] = s
            dn = send(scaled.at[t - 1], sabove.at[t - 1], below, 9 + 2 * (t - 1))
            up = send(scaled.at[t - 1], sbelow.at[t - 1], above, 10 + 2 * (t - 1))
            pending += [dn, up]
            dn.wait_recv()
            up.wait_recv()
            sa = jnp.where(has_above, sabove[t - 1], 0.0)
            lz = lz + HALF * (sa - s)
            lzl = lzl + HALF * (s - sbelow[t - 1])
            lx = lx + HALF * up_x(s)
            ly = ly + HALF * up_y(s)
            lp = keep * adj + HALF * (
                buoy * lz - b_low * lzl + down_x(buoy * lx) + down_y(buoy * ly))
    grad[0] = gk * (2.0 * dens[...] * speed[...])
    grad[1] = gd
    rows_out = 256 // n_grp
    copies = []
    for d in range(1, n_grp):
        peer = lax.rem(grp + d, n_grp)
        c = pltpu.make_async_remote_copy(
            src_ref=grad.at[:, pl.ds(pl.multiple_of(peer * rows_out, rows_out), rows_out)],
            dst_ref=gradrecv.at[d], send_sem=grad_send.at[d],
            recv_sem=grad_recv.at[d], device_id=(slab, peer), device_id_type=MESH)
        c.start()
        copies.append(c)
    total = grad[:, pl.ds(pl.multiple_of(grp * rows_out, rows_out), rows_out)]
    for d in range(1, n_grp):
        copies[d - 1].wait_recv()
        total = total + gradrecv[d]
    out_s[0] = total[0]
    out_a[0] = total[1]
    for c in [p0_down, w_up, b_up] + pending + copies:
        c.wait_send()


def shards(
    n_slab, n_grp,
    sound_speed, density, attenuation, wavelet, weights, emitter_group, emitter_cell,
    receiver_cell, pressure_start, velocity_start, observed,
):
    vmem = pl.BlockSpec(memory_space=pltpu.VMEM)
    hbm = pl.BlockSpec(memory_space=pl.ANY)
    smem = pl.BlockSpec(memory_space=pltpu.SMEM)
    rows = 256 // n_grp
    plane = lambda *n: pltpu.VMEM(n + (256, 256), F32)
    out = jax.ShapeDtypeStruct((1, rows, 256), F32)
    dma = pltpu.SemaphoreType.DMA
    return pl.pallas_call(
        functools.partial(kernel, n_slab, n_grp),
        out_shape=(out, out),
        in_specs=[smem] + [hbm] * 5 + [vmem] * 5,
        out_specs=(vmem, vmem),
        scratch_shapes=[
            plane(), plane(), plane(), plane(4), plane(3), plane(), plane(), plane(), plane(),
            plane(), plane(3), plane(3), plane(3), plane(3), plane(3),
            pltpu.VMEM((n_grp, 8, 128), F32), pltpu.VMEM((n_grp, 8, 128), F32),
            plane(2), pltpu.VMEM((n_grp, 2, rows, 256), F32),
            dma((5,)), dma((15,)), dma((15,)), dma((n_grp,)), dma((n_grp,)),
            dma((n_grp,)), dma((n_grp,)),
        ],
        compiler_params=pltpu.CompilerParams(
            collective_id=0, has_side_effects=True, vmem_limit_bytes=48 * 1024 * 1024),
    )(
        wavelet, sound_speed, density, attenuation, pressure_start, velocity_start, weights,
        emitter_group.reshape(1, -1), emitter_cell.reshape(1, -1),
        receiver_cell.reshape(1, -1), observed,
    )


def solution(mesh):
    return jax.shard_map(
        functools.partial(shards, mesh.shape["slab"], mesh.shape["grp"]),
        mesh=mesh,
        in_specs=(
            P("slab", None, None),
            P("slab", None, None),
            P("slab", None, None),
            P(),
            P(),
            P(),
            P(),
            P("slab"),
            P("grp", "slab", None, None),
            P(None, "grp", "slab", None, None),
            P("grp", None, "slab"),
        ),
        out_specs=(P("slab", "grp", None), P("slab", "grp", None)),
        check_vma=False,
    )
```

```python
import functools
import jax
import jax.numpy as jnp
from jax import lax
from jax.experimental import pallas as pl
from jax.experimental.pallas import tpu as pltpu
from jax.sharding import PartitionSpec as P

MESH = pl.DeviceIdType.MESH
HALF = 0.5
F32 = jnp.float32
BF16 = jnp.bfloat16


I16 = jnp.int16
I32 = jnp.int32
TOP = 32767.0
NT_DOT = (((1,), (1,)), ((), ()))


def split2(v):
    hi = v.astype(BF16)
    return hi, (v - hi.astype(F32)).astype(BF16)


def split3(v):
    hi = v.astype(BF16)
    rest = v - hi.astype(F32)
    mid = rest.astype(BF16)
    return hi, mid, (rest - mid.astype(F32)).astype(BF16)


def code(v):
    return jnp.round(v).astype(I32).astype(I16)


def decode(v):
    return v.astype(I32).astype(F32)


def code_root(v, top):
    root = jnp.sqrt(jnp.abs(v) * (1.0 / top)) * TOP
    return code(jnp.where(v < 0.0, -root, root))


def decode_root(v):
    u = decode(v)
    return u * jnp.abs(u)


def top_of(v):
    return jnp.max(jnp.max(jnp.abs(v), axis=0, keepdims=True), axis=1, keepdims=True)


P_MAX = 6.0
W_MAX = 7.3
B_MID = 1.0714286
B_MAX = 0.3573


def kernel(
    n_slab, n_grp,
    wav, speed_h, dens_h, atten_h, press_h, vel_h, weights_h, group_h, ecell_h, rcell_h, obs_h,
    out_s, out_a,
    speed, dens, atten, press, vel, weights, group, ecell, obs, rcs,
    p0_out, w_out, b_out, p1_out, s1_out, p0_in, w_in, b_in, p1_in, s1_in,
    p1_scale, p1_scale_in, p2_out, p2_in, far_out, far_in, part_out, part_in, fix_out, fix_in,
    res_out, res_in, s1_scale, s1_scale_in,
    encsend, encrecv, grad, coded, gradrecv, gscale, gscale_in,
    load_sem, halo_send, halo_recv, enc_send, enc_recv, grad_send, grad_recv, gs_send, gs_recv,
):
    steps = 4
    slab = lax.axis_index("slab")
    grp = lax.axis_index("grp")
    above = lax.rem(slab + 1, n_slab)
    below = lax.rem(slab + n_slab - 1, n_slab)

    loads = [
        pltpu.make_async_copy(src, dst, load_sem.at[i])
        for i, (src, dst) in enumerate([
            (press_h.at[0, 0], press.at[0]), (dens_h.at[0], dens), (vel_h.at[:, 0, 0], vel),
            (rcell_h, rcs.at[2]), (weights_h, weights), (group_h, group), (obs_h, obs),
            (ecell_h, ecell), (speed_h.at[0], speed), (atten_h.at[0], atten),
        ])
    ]
    for c in loads:
        c.start()

    near = {d: lax.rem(slab + n_slab + d, n_slab) for d in (-2, -1, 1, 2)}
    barrier = pltpu.get_barrier_semaphore()
    for s in near.values():
        pl.semaphore_signal(barrier, inc=1, device_id=(s, grp), device_id_type=MESH)
    for d in range(1, n_grp):
        pl.semaphore_signal(
            barrier, inc=1, device_id=(slab, lax.rem(grp + d, n_grp)), device_id_type=MESH)

    for c in loads[:3]:
        c.wait()
    p0_out[...] = code(press[0] * (TOP / P_MAX))
    buoy = 1.0 / dens[...]
    w_out[...] = code((vel[0] + HALF * buoy * press[0]) * (TOP / W_MAX))
    b_out[...] = code((buoy - B_MID) * (TOP / B_MAX))
    loads[3].wait()
    pl.semaphore_wait(barrier, n_grp + 3)

    pending = []

    def send(src, dst, to, k):
        c = pltpu.make_async_remote_copy(
            src_ref=src, dst_ref=dst, send_sem=halo_send.at[k], recv_sem=halo_recv.at[k],
            device_id=(to, grp), device_id_type=MESH)
        c.start()
        pending.append(c)
        return c

    cells = [send(rcs.at[2], rcs.at[2 - d], near[d], i) for i, d in enumerate((-2, -1, 1, 2))]
    p0_down = send(p0_out, p0_in, below, 4)
    w_up = send(w_out, w_in, above, 5)
    b_up = send(b_out, b_in, above, 6)

    for c in loads[4:7]:
        c.wait()
    e_dev = obs.shape[0]
    eoff = pl.multiple_of(grp * e_dev, 128)
    wdev = weights[:, pl.ds(eoff, e_dev)].astype(F32)
    gdev = group[:, pl.ds(eoff, e_dev)]
    act_dev = jnp.where(
        gdev == lax.broadcasted_iota(I32, wdev.shape, 0), wdev, 0.0).astype(BF16)
    er = lax.broadcasted_iota(I32, (e_dev, e_dev * steps), 0)
    el = lax.broadcasted_iota(I32, (e_dev, e_dev * steps), 1)
    expand = jnp.where((el >> 2) == er, 1.0, 0.0).astype(BF16)
    wide = jnp.dot(act_dev, expand, preferred_element_type=F32).astype(BF16)
    rr = lax.broadcasted_iota(I32, (8 * n_grp, n_grp), 0)
    rl = lax.broadcasted_iota(I32, (8 * n_grp, n_grp), 1)
    rows = jnp.where((rr >> 3) == rl, 1.0, 0.0).astype(BF16)
    tall = jnp.dot(rows, wide, preferred_element_type=F32)
    tr = lax.broadcasted_iota(I32, tall.shape, 0)
    tl = lax.broadcasted_iota(I32, tall.shape, 1)
    lhs = jnp.where((tr & 7) == (tl & 3), tall, 0.0).astype(BF16)
    flat = obs[...].astype(F32).reshape(e_dev * steps, obs.shape[2]).astype(BF16)
    part = jnp.dot(lhs, flat, preferred_element_type=F32)
    encsend[...] = part.reshape(encsend.shape)
    enc_copies = []
    for d in range(1, n_grp):
        peer = lax.rem(grp + d, n_grp)
        c = pltpu.make_async_remote_copy(
            src_ref=encsend.at[peer], dst_ref=encrecv.at[d], send_sem=enc_send.at[d],
            recv_sem=enc_recv.at[d], device_id=(slab, peer), device_id_type=MESH)
        c.start()
        enc_copies.append(c)
    pending += enc_copies

    loads[7].wait()
    wall = weights[...].astype(F32)
    shot_row = lax.broadcasted_iota(I32, wall.shape, 0)
    own = jnp.sum(
        jnp.where((group[...] == shot_row) & (shot_row == grp), wall, 0.0),
        axis=0, keepdims=True)
    emit = wall.shape[1]
    ec = ecell[...] - slab * 65536
    ex = jnp.where((ec >= 0) & (ec < 65536), ec >> 8, -1)
    row_e = lax.broadcasted_iota(I32, (256, emit), 0)
    ax = jnp.where(row_e == ex, own, 0.0).astype(BF16)
    ay = jnp.where(row_e == (ec & 255), 1.0, 0.0).astype(BF16)
    amp = lax.dot_general(ax, ay, NT_DOT, preferred_element_type=F32)

    for c in cells:
        c.wait_recv()
    row_r = lax.broadcasted_iota(I32, (256, 128), 0)
    col_x, hot_y = {}, {}
    for d in range(-2, 3):
        rc = rcs[d + 2]
        inside = (slab + d >= 0) & (slab + d < n_slab)
        col_x[d] = jnp.where(inside, rc >> 8, -1000)
        y = jnp.where(inside, rc & 255, -1000)
        for dy in (-1, 0, 1) if abs(d) < 2 else (0,):
            hot_y[d, dy] = jnp.where(row_r == y + dy, 1.0, 0.0).astype(BF16)

    star = ((0, -1), (-1, 0), (0, 0), (1, 0), (0, 1))

    def spots(d, others):
        return [(d, dx, dy) for dx, dy in star] + [(o, 0, 0) for o in others]

    def blocks(points):
        return sorted({(d, dy) for d, _, dy in points})

    def gather(pieces, points):
        table = {}
        for key in blocks(points):
            table[key] = sum(
                jnp.dot(piece, hot_y[key], preferred_element_type=F32) for piece in pieces)
        return [
            jnp.sum(jnp.where(row_r == col_x[d] + dx, table[d, dy], 0.0), axis=0, keepdims=True)
            for d, dx, dy in points
        ]

    def scatter(values, points, split):
        left = []
        keys = blocks(points)
        for key in keys:
            total = 0.0
            for v, (d, dx, dy) in zip(values, points):
                if (d, dy) == key:
                    total = total + jnp.where(row_r == col_x[d] + dx, v, 0.0)
            left.append(total)
        right = [hot_y[key] for key in keys]
        pieces = [split(x) for x in left]
        count = len(pieces[0])
        lhs = jnp.concatenate([pc[i] for i in range(count) for pc in pieces], axis=1)
        rhs = jnp.concatenate(right * count, axis=1)
        return lax.dot_general(lhs, rhs, NT_DOT, preferred_element_type=F32)

    def column(rows_list):
        pad = 8 - len(rows_list)
        if pad:
            rows_list = rows_list + [jnp.zeros((pad, 128), F32)]
        return jnp.concatenate(rows_list, axis=0)

    only = [(0, 0, 0)]
    ring = spots(0, (1, -1))
    ones = jnp.ones((1, 128), F32)
    plain = lambda v: (v.astype(BF16),)
    count = scatter([ones] * 7, ring, plain)
    inv_ring = jnp.where(count > 0.5, 1.0 / count, 0.0)

    xi = lax.broadcasted_iota(I32, (256, 256), 0)
    yi = lax.broadcasted_iota(I32, (256, 256), 1)

    def up_x(f):
        return jnp.where(xi == 255, 0.0, pltpu.roll(f, 255, 0)) - f

    def up_y(f):
        return jnp.where(yi == 255, 0.0, pltpu.roll(f, 255, 1)) - f

    def down_x(f):
        return f - jnp.where(xi == 0, 0.0, pltpu.roll(f, 1, 0))

    def down_y(f):
        return f - jnp.where(yi == 0, 0.0, pltpu.roll(f, 1, 1))

    has_above = slab < n_slab - 1
    has_below = slab > 0
    for c in loads[8:]:
        c.wait()
    kappa = dens[...] * speed[...] * speed[...]
    keep = 1.0 - atten[...]
    hk = HALF * kappa
    hb = HALF * buoy

    def local_step(p, px, py):
        px = px - hb * up_x(p)
        py = py - hb * up_y(p)
        return px, py, down_x(px) + down_y(py)

    divs = [None] * steps
    recorded = [None] * steps
    p = press[0]
    px, py, flat_div = local_step(p, vel[1], vel[2])
    pz = vel[0] + hb * p
    base = keep * p + wav[0] * amp

    nearby = [(1, 0, 0), (-1, 0, 0)]
    kappa_at = gather(split2(kappa), spots(0, (1, -1)))
    buoy_at = gather(split2(buoy), [(0, 0, 0), (0, -1, 0), (0, 0, -1)] + nearby)
    keep_at = gather(split2(keep), only)[0]
    amp_at = gather(split3(amp), only)[0]

    p0_down.wait_recv()
    w_up.wait_recv()
    b_up.wait_recv()
    b_low = jnp.where(has_below, decode(b_in[...]) * (B_MAX / TOP) + B_MID, 0.0)
    hbl = HALF * b_low
    pzl = jnp.where(has_below, decode(w_in[...]) * (W_MAX / TOP), 0.0) - hbl * p
    pz = pz - hb * jnp.where(has_above, decode(p0_in[...]) * (P_MAX / TOP), 0.0)
    divs[0] = pz - pzl + flat_div
    p = base - hk * divs[0]
    press[1] = p

    top = jnp.maximum(top_of(p), 1e-30)
    p1_out[...] = code(p * (TOP / top))
    p1_scale[...] = jnp.broadcast_to(top * (1.0 / TOP), (8, 128))
    got = [
        send(p1_out, p1_in.at[0], below, 7), send(p1_out, p1_in.at[1], above, 8),
        send(p1_scale, p1_scale_in.at[0], below, 9),
        send(p1_scale, p1_scale_in.at[1], above, 10)]

    low_at = gather(split2(b_low), only + nearby)
    fix_out[...] = column([
        0.25 * kappa_at[5] * buoy_at[3], 0.25 * kappa_at[5] * low_at[1],
        0.25 * kappa_at[6] * buoy_at[4], 0.25 * kappa_at[6] * low_at[2]])
    fixed = [
        send(fix_out, fix_in.at[0], below, 11), send(fix_out, fix_in.at[1], above, 12)]
    k_at, b_at = kappa_at[2], buoy_at[0]
    own_at = 0.25 * k_at * b_at
    star_at = [
        kappa_at[0] * 0.25 * k_at * buoy_at[2],
        kappa_at[1] * 0.25 * k_at * buoy_at[1],
        k_at * (keep_at - 0.25 * k_at * (3.0 * b_at + buoy_at[1] + buoy_at[2] + low_at[0])),
        kappa_at[3] * own_at,
        kappa_at[4] * own_at]

    recorded[0] = gather(split3(p), only)[0]
    px, py, flat_div = local_step(p, px, py)
    pz = pz + hb * p
    pzl = pzl - hbl * p
    base = keep * p + wav[1] * amp
    for c in got:
        c.wait_recv()
    pz = pz - hb * jnp.where(has_above, decode(p1_in[0]) * p1_scale_in[0, 0:1, 0:1], 0.0)
    pzl = pzl + hbl * (decode(p1_in[1]) * p1_scale_in[1, 0:1, 0:1])
    divs[1] = pz - pzl + flat_div
    p = base - hk * divs[1]
    press[2] = p

    to_up, to_down = spots(1, (0, 2)), spots(-1, (0, -2))
    values = gather(split2(p), to_up + to_down)
    p2_out[0] = column(values[7:])
    p2_out[1] = column(values[:7])
    far_out[0] = column(values[13:])
    far_out[1] = column(values[6:7])
    got = [
        send(p2_out.at[0], p2_in.at[0], below, 13), send(p2_out.at[1], p2_in.at[1], above, 14)]
    far = [
        send(far_out.at[0], far_in.at[0], near[-2], 15),
        send(far_out.at[1], far_in.at[1], near[2], 16)]
    px, py, flat_div = local_step(p, px, py)
    pz = pz + hb * p
    pzl = pzl - hbl * p
    flat_div = pz - pzl + flat_div
    base = keep * p + wav[2] * amp - hk * flat_div
    values = gather(split2(base), nearby)
    part_out[0] = column(values[1:])
    part_out[1] = column(values[:1])
    parts = [
        send(part_out.at[0], part_in.at[0], below, 17),
        send(part_out.at[1], part_in.at[1], above, 18)]
    recorded[1] = gather(split3(p), only)[0]
    for c in got:
        c.wait_recv()
    ua = hb * (inv_ring * scatter(
        [p2_in[0, i:i + 1] for i in range(7)], spots(0, (1, -1)), split2))
    ub = hbl * (inv_ring * scatter(
        [p2_in[1, i:i + 1] for i in range(7)], spots(0, (-1, 1)), split2))
    pz = pz - ua
    pzl = pzl + ub
    divs[2] = flat_div - ua - ub
    p = base + hk * (ua + ub)
    press[3] = p
    recorded[2] = gather(split3(p), only)[0]

    px, py, flat_div = local_step(p, px, py)
    div_at = gather(split3(pz + hb * p - (pzl - hbl * p) + flat_div), only)[0]
    for c in far + fixed + parts:
        c.wait_recv()
    pa = part_in[0, 0:1] + fix_in[0, 2:3] * far_in[0, 0:1] + fix_in[0, 3:4] * recorded[1]
    pb = part_in[1, 0:1] + fix_in[1, 0:1] * recorded[1] + fix_in[1, 1:2] * far_in[1, 0:1]
    pa = jnp.where(has_above, pa, 0.0)
    div_at = div_at - HALF * (b_at * pa + low_at[0] * pb)
    recorded[3] = keep_at * recorded[2] - HALF * k_at * div_at + wav[3] * amp_at

    for c in enc_copies:
        c.wait_recv()
    enc = encsend[grp]
    for d in range(1, n_grp):
        enc = enc + encrecv[d]
    res = [(recorded[t] - enc[t:t + 1]) * (1.0 / n_grp) for t in range(steps)]

    sigma = k_at * res[3]
    star_rows = [v * res[3] for v in star_at]
    star_rows[2] = star_rows[2] + k_at * res[2]
    res_out[...] = column([sigma] + star_rows)
    got = [
        send(res_out, res_in.at[0], below, 19), send(res_out, res_in.at[1], above, 20),
        send(res_out, res_in.at[2], near[-2], 21), send(res_out, res_in.at[3], near[2], 22)]

    adj = scatter([res[3]], only, split3)
    gd = -adj * press[3]
    gk = scatter([-HALF * res[3] * div_at], only, split3)
    inj = [scatter([res[t]], only, split3) for t in range(steps - 1)]
    s = kappa * adj
    lz = -HALF * s
    lzl = HALF * s
    lx = HALF * up_x(s)
    ly = HALF * up_y(s)
    base = keep * adj + HALF * (down_x(buoy * lx) + down_y(buoy * ly)) + inj[2]
    for c in got:
        c.wait_recv()
    lz = lz + HALF * scatter([res_in[0, 0:1]], [(1, 0, 0)], split2)
    lzl = lzl - HALF * scatter([res_in[1, 0:1]], [(-1, 0, 0)], split2)
    adj = base + hb * lz - hbl * lzl
    sa = scatter(
        [res_in[0, i:i + 1] for i in range(1, 6)]
        + [fix_in[0, 0:1] * res_in[2, 0:1], fix_in[0, 3:4] * sigma],
        spots(1, (2, 0)), split2)
    sb = scatter(
        [res_in[1, i:i + 1] for i in range(1, 6)]
        + [fix_in[1, 0:1] * sigma, fix_in[1, 3:4] * res_in[3, 0:1]],
        spots(-1, (0, -2)), split2)
    gd = gd - adj * press[2]
    gk = gk - HALF * adj * divs[2]
    s = kappa * adj
    lz = lz + HALF * (sa - s)
    lzl = lzl + HALF * (s - sb)
    lx = lx + HALF * up_x(s)
    ly = ly + HALF * up_y(s)
    adj = inj[1] + keep * adj + (
        hb * lz - hbl * lzl + HALF * (down_x(buoy * lx) + down_y(buoy * ly)))
    s = kappa * adj
    top = jnp.maximum(top_of(s), 1e-30)
    s1_out[...] = code_root(s, top)
    s1_scale[...] = jnp.broadcast_to(top * (1.0 / (TOP * TOP)), (8, 128))
    got = [
        send(s1_out, s1_in.at[0], below, 23), send(s1_out, s1_in.at[1], above, 24),
        send(s1_scale, s1_scale_in.at[0], below, 25),
        send(s1_scale, s1_scale_in.at[1], above, 26)]
    gd = gd - adj * press[1]
    gk = gk - HALF * adj * divs[1]
    lz = lz - HALF * s
    lzl = lzl + HALF * s
    lx = lx + HALF * up_x(s)
    ly = ly + HALF * up_y(s)
    adj = inj[0] + keep * adj + (
        hb * lz - hbl * lzl + HALF * (down_x(buoy * lx) + down_y(buoy * ly)))
    for c in got:
        c.wait_recv()
    sa = jnp.where(has_above, decode_root(s1_in[0]) * s1_scale_in[0, 0:1, 0:1], 0.0)
    sb = decode_root(s1_in[1]) * s1_scale_in[1, 0:1, 0:1]
    adj = adj + HALF * (hb * sa + hbl * sb)
    gd = gd - adj * press[0]
    gk = gk - HALF * adj * divs[0]
    gk = gk * (2.0 * dens[...] * speed[...])
    for i, g in enumerate((gk, gd)):
        grad[i] = g
        top = jnp.maximum(top_of(g), 1e-30)
        coded[i] = code_root(g, top)
        gscale[i] = jnp.broadcast_to(top * (1.0 / (TOP * TOP)), (8, 128))
    rows_out = 256 // n_grp
    copies = []
    for d in range(1, n_grp):
        peer = lax.rem(grp + d, n_grp)
        c = pltpu.make_async_remote_copy(
            src_ref=coded.at[:, pl.ds(pl.multiple_of(peer * rows_out, rows_out), rows_out)],
            dst_ref=gradrecv.at[d], send_sem=grad_send.at[d],
            recv_sem=grad_recv.at[d], device_id=(slab, peer), device_id_type=MESH)
        c.start()
        e = pltpu.make_async_remote_copy(
            src_ref=gscale, dst_ref=gscale_in.at[d], send_sem=gs_send.at[d],
            recv_sem=gs_recv.at[d], device_id=(slab, peer), device_id_type=MESH)
        e.start()
        copies.append((c, e))
    mine = pl.ds(pl.multiple_of(grp * rows_out, rows_out), rows_out)
    total = [grad[0, mine], grad[1, mine]]
    for d in range(1, n_grp):
        for c in copies[d - 1]:
            c.wait_recv()
        for i in range(2):
            total[i] = total[i] + decode_root(gradrecv[d, i]) * gscale_in[d, i, 0:1, 0:1]
    out_s[0] = total[0]
    out_a[0] = total[1]
    for c in pending + [c for pair in copies for c in pair]:
        c.wait_send()


def shards(
    n_slab, n_grp,
    sound_speed, density, attenuation, wavelet, weights, emitter_group, emitter_cell,
    receiver_cell, pressure_start, velocity_start, observed,
):
    vmem = pl.BlockSpec(memory_space=pltpu.VMEM)
    hbm = pl.BlockSpec(memory_space=pltpu.HBM)
    smem = pl.BlockSpec(memory_space=pltpu.SMEM)
    rows = 256 // n_grp
    plane = lambda *n, t=F32: pltpu.VMEM(n + (256, 256), t)
    tile = lambda *n: pltpu.VMEM(n + (8, 128), F32)
    out = jax.ShapeDtypeStruct((1, rows, 256), F32)
    dma = pltpu.SemaphoreType.DMA
    emit = weights.shape[1]
    return pl.pallas_call(
        functools.partial(kernel, n_slab, n_grp),
        out_shape=(out, out),
        in_specs=[smem] + [hbm] * 10,
        out_specs=(vmem, vmem),
        scratch_shapes=[
            plane(), plane(), plane(), plane(4), plane(3),
            pltpu.VMEM(weights.shape, BF16), pltpu.VMEM((1, emit), I32),
            pltpu.VMEM((1, emit), I32), pltpu.VMEM(observed.shape, BF16),
            pltpu.VMEM((5, 1, 128), I32),
            plane(t=I16), plane(t=I16), plane(t=I16), plane(t=I16), plane(t=I16),
            plane(t=I16), plane(t=I16), plane(t=I16), plane(2, t=I16), plane(2, t=I16),
            tile(), tile(2), tile(2), tile(2), tile(2), tile(2), tile(2), tile(2), tile(), tile(2),
            tile(), tile(4), tile(), tile(2),
            tile(n_grp), tile(n_grp), plane(2), plane(2, t=I16),
            pltpu.VMEM((n_grp, 2, rows, 256), I16), tile(2), tile(n_grp, 2),
            dma((10,)), dma((27,)), dma((27,)), dma((n_grp,)), dma((n_grp,)),
            dma((n_grp,)), dma((n_grp,)), dma((n_grp,)), dma((n_grp,)),
        ],
        compiler_params=pltpu.CompilerParams(
            collective_id=0, has_side_effects=True, vmem_limit_bytes=60 * 1024 * 1024),
    )(
        wavelet, sound_speed, density, attenuation, pressure_start, velocity_start, weights,
        emitter_group.reshape(1, -1), emitter_cell.reshape(1, -1),
        receiver_cell.reshape(1, -1), observed,
    )


def solution(mesh):
    return jax.shard_map(
        functools.partial(shards, mesh.shape["slab"], mesh.shape["grp"]),
        mesh=mesh,
        in_specs=(
            P("slab", None, None),
            P("slab", None, None),
            P("slab", None, None),
            P(),
            P(),
            P(),
            P(),
            P("slab"),
            P("grp", "slab", None, None),
            P(None, "grp", "slab", None, None),
            P("grp", None, "slab"),
        ),
        out_specs=(P("slab", "grp", None), P("slab", "grp", None)),
        check_vma=False,
    )
```

```python
import functools
import jax
import jax.numpy as jnp
from jax import lax
from jax.experimental import pallas as pl
from jax.experimental.pallas import tpu as pltpu
from jax.sharding import PartitionSpec as P

MESH = pl.DeviceIdType.MESH
HALF = 0.5
F32 = jnp.float32
BF16 = jnp.bfloat16


I16 = jnp.int16
I32 = jnp.int32
TOP = 32767.0
NT_DOT = (((1,), (1,)), ((), ()))


def split2(v):
    hi = v.astype(BF16)
    return hi, (v - hi.astype(F32)).astype(BF16)


def split3(v):
    hi = v.astype(BF16)
    rest = v - hi.astype(F32)
    mid = rest.astype(BF16)
    return hi, mid, (rest - mid.astype(F32)).astype(BF16)


def code(v):
    return jnp.round(v).astype(I32).astype(I16)


def decode(v):
    return v.astype(I32).astype(F32)


def code_root(v, top):
    root = jnp.sqrt(jnp.abs(v) * (1.0 / top)) * TOP
    return code(jnp.where(v < 0.0, -root, root))


def decode_root(v):
    u = decode(v)
    return u * jnp.abs(u)


def top_of(v):
    return jnp.max(jnp.max(jnp.abs(v), axis=0, keepdims=True), axis=1, keepdims=True)


P_MAX = 6.0
W_MAX = 7.3
B_MID = 1.0714286
B_MAX = 0.3573
K_MID = 0.7875
K_MAX = 0.6127
D_MID = 0.895
D_MAX = 0.0952


def kernel(
    n_slab, n_grp,
    wav, speed_h, dens_h, atten_h, press_h, vel_h, weights_h, group_h, ecell_h, rcell_h, obs_h,
    out_s, out_a,
    speed, dens, atten, press, vel, weights, group, ecell, obs, rcs,
    p0_out, w_out, b_out, p1_out, p0_in, w_in, b_in, p1_in,
    p1_scale, p1_scale_in, p2_out, p2_in, far_out, far_in, part_out, part_in, fix_out, fix_in,
    res_out, res_in, fix2_in, k_out, k_in, d_out, d_in, b2_in,
    encsend, encrecv, grad, coded, gradrecv, gscale, gscale_in,
    load_sem, halo_send, halo_recv, enc_send, enc_recv, grad_send, grad_recv, gs_send, gs_recv,
):
    steps = 4
    slab = lax.axis_index("slab")
    grp = lax.axis_index("grp")
    above = lax.rem(slab + 1, n_slab)
    below = lax.rem(slab + n_slab - 1, n_slab)

    loads = [
        pltpu.make_async_copy(src, dst, load_sem.at[i])
        for i, (src, dst) in enumerate([
            (press_h.at[0, 0], press.at[0]), (dens_h.at[0], dens), (vel_h.at[:, 0, 0], vel),
            (rcell_h, rcs.at[3]), (weights_h, weights), (group_h, group), (obs_h, obs),
            (ecell_h, ecell), (speed_h.at[0], speed), (atten_h.at[0], atten),
        ])
    ]
    for c in loads:
        c.start()

    near = {d: lax.rem(slab + n_slab + d, n_slab) for d in (-3, -2, -1, 1, 2, 3)}
    barrier = pltpu.get_barrier_semaphore()
    for s in near.values():
        pl.semaphore_signal(barrier, inc=1, device_id=(s, grp), device_id_type=MESH)
    for d in range(1, n_grp):
        pl.semaphore_signal(
            barrier, inc=1, device_id=(slab, lax.rem(grp + d, n_grp)), device_id_type=MESH)

    for c in loads[:3]:
        c.wait()
    p0_out[...] = code(press[0] * (TOP / P_MAX))
    buoy = 1.0 / dens[...]
    w_out[...] = code((vel[0] + HALF * buoy * press[0]) * (TOP / W_MAX))
    b_out[...] = code((buoy - B_MID) * (TOP / B_MAX))
    loads[3].wait()
    pl.semaphore_wait(barrier, n_grp + 5)

    pending = []

    def send(src, dst, to, k):
        c = pltpu.make_async_remote_copy(
            src_ref=src, dst_ref=dst, send_sem=halo_send.at[k], recv_sem=halo_recv.at[k],
            device_id=(to, grp), device_id_type=MESH)
        c.start()
        pending.append(c)
        return c

    cells = [send(rcs.at[3], rcs.at[3 - d], near[d], 27 + d) for d in near]
    p0_down = send(p0_out, p0_in, below, 4)
    w_up = send(w_out, w_in, above, 5)
    b_up = send(b_out, b_in, above, 6)

    for c in loads[4:7]:
        c.wait()
    e_dev = obs.shape[0]
    eoff = pl.multiple_of(grp * e_dev, 128)
    wdev = weights[:, pl.ds(eoff, e_dev)].astype(F32)
    gdev = group[:, pl.ds(eoff, e_dev)]
    act_dev = jnp.where(
        gdev == lax.broadcasted_iota(I32, wdev.shape, 0), wdev, 0.0).astype(BF16)
    er = lax.broadcasted_iota(I32, (e_dev, e_dev * steps), 0)
    el = lax.broadcasted_iota(I32, (e_dev, e_dev * steps), 1)
    expand = jnp.where((el >> 2) == er, 1.0, 0.0).astype(BF16)
    wide = jnp.dot(act_dev, expand, preferred_element_type=F32).astype(BF16)
    rr = lax.broadcasted_iota(I32, (8 * n_grp, n_grp), 0)
    rl = lax.broadcasted_iota(I32, (8 * n_grp, n_grp), 1)
    rows = jnp.where((rr >> 3) == rl, 1.0, 0.0).astype(BF16)
    tall = jnp.dot(rows, wide, preferred_element_type=F32)
    tr = lax.broadcasted_iota(I32, tall.shape, 0)
    tl = lax.broadcasted_iota(I32, tall.shape, 1)
    lhs = jnp.where((tr & 7) == (tl & 3), tall, 0.0).astype(BF16)
    flat = obs[...].astype(F32).reshape(e_dev * steps, obs.shape[2]).astype(BF16)
    part = jnp.dot(lhs, flat, preferred_element_type=F32)
    encsend[...] = part.reshape(encsend.shape)
    enc_copies = []
    for d in range(1, n_grp):
        peer = lax.rem(grp + d, n_grp)
        c = pltpu.make_async_remote_copy(
            src_ref=encsend.at[peer], dst_ref=encrecv.at[d], send_sem=enc_send.at[d],
            recv_sem=enc_recv.at[d], device_id=(slab, peer), device_id_type=MESH)
        c.start()
        enc_copies.append(c)
    pending += enc_copies

    loads[7].wait()
    wall = weights[...].astype(F32)
    shot_row = lax.broadcasted_iota(I32, wall.shape, 0)
    own = jnp.sum(
        jnp.where((group[...] == shot_row) & (shot_row == grp), wall, 0.0),
        axis=0, keepdims=True)
    emit = wall.shape[1]
    ec = ecell[...] - slab * 65536
    ex = jnp.where((ec >= 0) & (ec < 65536), ec >> 8, -1)
    row_e = lax.broadcasted_iota(I32, (256, emit), 0)
    ax = jnp.where(row_e == ex, own, 0.0).astype(BF16)
    ay = jnp.where(row_e == (ec & 255), 1.0, 0.0).astype(BF16)
    amp = lax.dot_general(ax, ay, NT_DOT, preferred_element_type=F32)

    for c in cells:
        c.wait_recv()
    row_r = lax.broadcasted_iota(I32, (256, 128), 0)
    col_x, hot_y = {}, {}
    for d in range(-3, 4):
        rc = rcs[d + 3]
        inside = (slab + d >= 0) & (slab + d < n_slab)
        col_x[d] = jnp.where(inside, rc >> 8, -1000)
        y = jnp.where(inside, rc & 255, -1000)
        for dy in (-1, 0, 1) if abs(d) < 3 else (0,):
            hot_y[d, dy] = jnp.where(row_r == y + dy, 1.0, 0.0).astype(BF16)

    star = ((0, -1), (-1, 0), (0, 0), (1, 0), (0, 1))

    def spots(d, others):
        return [(d, dx, dy) for dx, dy in star] + [(o, 0, 0) for o in others]

    def blocks(points):
        return sorted({(d, dy) for d, _, dy in points})

    def gather(pieces, points):
        table = {}
        for key in blocks(points):
            table[key] = sum(
                jnp.dot(piece, hot_y[key], preferred_element_type=F32) for piece in pieces)
        return [
            jnp.sum(jnp.where(row_r == col_x[d] + dx, table[d, dy], 0.0), axis=0, keepdims=True)
            for d, dx, dy in points
        ]

    def scatter(values, points, split):
        left = []
        keys = blocks(points)
        for key in keys:
            total = 0.0
            for v, (d, dx, dy) in zip(values, points):
                if (d, dy) == key:
                    total = total + jnp.where(row_r == col_x[d] + dx, v, 0.0)
            left.append(total)
        right = [hot_y[key] for key in keys]
        pieces = [split(x) for x in left]
        count = len(pieces[0])
        lhs = jnp.concatenate([pc[i] for i in range(count) for pc in pieces], axis=1)
        rhs = jnp.concatenate(right * count, axis=1)
        return lax.dot_general(lhs, rhs, NT_DOT, preferred_element_type=F32)

    def column(rows_list):
        pad = 8 - len(rows_list)
        if pad:
            rows_list = rows_list + [jnp.zeros((pad, 128), F32)]
        return jnp.concatenate(rows_list, axis=0)

    only = [(0, 0, 0)]
    ring = spots(0, (1, -1))
    ones = jnp.ones((1, 128), F32)
    plain = lambda v: (v.astype(BF16),)
    count = scatter([ones] * 7, ring, plain)
    inv_ring = jnp.where(count > 0.5, 1.0 / count, 0.0)

    xi = lax.broadcasted_iota(I32, (256, 256), 0)
    yi = lax.broadcasted_iota(I32, (256, 256), 1)

    def up_x(f):
        return jnp.where(xi == 255, 0.0, pltpu.roll(f, 255, 0)) - f

    def up_y(f):
        return jnp.where(yi == 255, 0.0, pltpu.roll(f, 255, 1)) - f

    def down_x(f):
        return f - jnp.where(xi == 0, 0.0, pltpu.roll(f, 1, 0))

    def down_y(f):
        return f - jnp.where(yi == 0, 0.0, pltpu.roll(f, 1, 1))

    has_above = slab < n_slab - 1
    has_below = slab > 0
    for c in loads[8:]:
        c.wait()
    kappa = dens[...] * speed[...] * speed[...]
    keep = 1.0 - atten[...]
    hk = HALF * kappa
    hb = HALF * buoy

    def local_step(p, px, py):
        px = px - hb * up_x(p)
        py = py - hb * up_y(p)
        return px, py, down_x(px) + down_y(py)

    divs = [None] * steps
    recorded = [None] * steps
    p = press[0]
    px, py, flat_div = local_step(p, vel[1], vel[2])
    pz = vel[0] + hb * p
    base = keep * p + wav[0] * amp

    nearby = [(1, 0, 0), (-1, 0, 0)]
    kappa_at = gather(split2(kappa), spots(0, (1, -1)))
    buoy_at = gather(split2(buoy), [(0, 0, 0), (0, -1, 0), (0, 0, -1)] + nearby)
    keep_at = gather(split2(keep), only)[0]
    amp_at = gather(split3(amp), only)[0]

    p0_down.wait_recv()
    w_up.wait_recv()
    b_up.wait_recv()
    b_low = jnp.where(has_below, decode(b_in[...]) * (B_MAX / TOP) + B_MID, 0.0)
    hbl = HALF * b_low
    pzl = jnp.where(has_below, decode(w_in[...]) * (W_MAX / TOP), 0.0) - hbl * p
    pz = pz - hb * jnp.where(has_above, decode(p0_in[...]) * (P_MAX / TOP), 0.0)
    divs[0] = pz - pzl + flat_div
    p = base - hk * divs[0]
    press[1] = p

    top = jnp.maximum(top_of(p), 1e-30)
    p1_out[...] = code(p * (TOP / top))
    p1_scale[...] = jnp.broadcast_to(top * (1.0 / TOP), (8, 128))
    got = [
        send(p1_out, p1_in.at[0], below, 7), send(p1_out, p1_in.at[1], above, 8),
        send(p1_scale, p1_scale_in.at[0], below, 9),
        send(p1_scale, p1_scale_in.at[1], above, 10)]

    k_out[...] = code((kappa - K_MID) * (TOP / K_MAX))
    d_out[...] = code((keep - D_MID) * (TOP / D_MAX))
    planes = [
        send(k_out, k_in.at[0], below, 0), send(k_out, k_in.at[1], above, 1),
        send(d_out, d_in.at[0], below, 2), send(d_out, d_in.at[1], above, 3)]
    low_at = gather(split2(b_low), only + nearby)
    fix_out[...] = column([
        0.25 * kappa_at[5] * buoy_at[3], 0.25 * kappa_at[5] * low_at[1],
        0.25 * kappa_at[6] * buoy_at[4], 0.25 * kappa_at[6] * low_at[2]])
    fixed = [
        send(fix_out, fix_in.at[0], below, 11), send(fix_out, fix_in.at[1], above, 12),
        send(fix_out, fix2_in.at[0], near[-2], 31), send(fix_out, fix2_in.at[1], near[2], 32)]
    k_at, b_at = kappa_at[2], buoy_at[0]
    own_at = 0.25 * k_at * b_at
    star_at = [
        kappa_at[0] * 0.25 * k_at * buoy_at[2],
        kappa_at[1] * 0.25 * k_at * buoy_at[1],
        k_at * (keep_at - 0.25 * k_at * (3.0 * b_at + buoy_at[1] + buoy_at[2] + low_at[0])),
        kappa_at[3] * own_at,
        kappa_at[4] * own_at]

    recorded[0] = gather(split3(p), only)[0]
    px, py, flat_div = local_step(p, px, py)
    pz = pz + hb * p
    pzl = pzl - hbl * p
    base = keep * p + wav[1] * amp
    for c in got:
        c.wait_recv()
    pz = pz - hb * jnp.where(has_above, decode(p1_in[0]) * p1_scale_in[0, 0:1, 0:1], 0.0)
    pzl = pzl + hbl * (decode(p1_in[1]) * p1_scale_in[1, 0:1, 0:1])
    divs[1] = pz - pzl + flat_div
    p = base - hk * divs[1]
    press[2] = p

    to_up, to_down = spots(1, (0, 2)), spots(-1, (0, -2))
    values = gather(split2(p), to_up + to_down)
    p2_out[0] = column(values[7:])
    p2_out[1] = column(values[:7])
    far_out[0] = column(values[13:])
    far_out[1] = column(values[6:7])
    got = [
        send(p2_out.at[0], p2_in.at[0], below, 13), send(p2_out.at[1], p2_in.at[1], above, 14)]
    far = [
        send(far_out.at[0], far_in.at[0], near[-2], 15),
        send(far_out.at[1], far_in.at[1], near[2], 16)]
    planes += [send(b_out, b2_in.at[0], below, 33), send(b_out, b2_in.at[1], near[2], 34)]
    px, py, flat_div = local_step(p, px, py)
    pz = pz + hb * p
    pzl = pzl - hbl * p
    flat_div = pz - pzl + flat_div
    base = keep * p + wav[2] * amp - hk * flat_div
    values = gather(split2(base), nearby)
    part_out[0] = column(values[1:])
    part_out[1] = column(values[:1])
    parts = [
        send(part_out.at[0], part_in.at[0], below, 17),
        send(part_out.at[1], part_in.at[1], above, 18)]
    recorded[1] = gather(split3(p), only)[0]
    for c in got:
        c.wait_recv()
    ua = hb * (inv_ring * scatter(
        [p2_in[0, i:i + 1] for i in range(7)], spots(0, (1, -1)), split2))
    ub = hbl * (inv_ring * scatter(
        [p2_in[1, i:i + 1] for i in range(7)], spots(0, (-1, 1)), split2))
    pz = pz - ua
    pzl = pzl + ub
    divs[2] = flat_div - ua - ub
    p = base + hk * (ua + ub)
    press[3] = p
    recorded[2] = gather(split3(p), only)[0]

    px, py, flat_div = local_step(p, px, py)
    div_at = gather(split3(pz + hb * p - (pzl - hbl * p) + flat_div), only)[0]
    for c in far + fixed + parts:
        c.wait_recv()
    pa = part_in[0, 0:1] + fix_in[0, 2:3] * far_in[0, 0:1] + fix_in[0, 3:4] * recorded[1]
    pb = part_in[1, 0:1] + fix_in[1, 0:1] * recorded[1] + fix_in[1, 1:2] * far_in[1, 0:1]
    pa = jnp.where(has_above, pa, 0.0)
    div_at = div_at - HALF * (b_at * pa + low_at[0] * pb)
    recorded[3] = keep_at * recorded[2] - HALF * k_at * div_at + wav[3] * amp_at

    for c in enc_copies:
        c.wait_recv()
    enc = encsend[grp]
    for d in range(1, n_grp):
        enc = enc + encrecv[d]
    res = [(recorded[t] - enc[t:t + 1]) * (1.0 / n_grp) for t in range(steps)]

    sigma = k_at * res[3]
    star_rows = [v * res[3] for v in star_at]
    star_rows[2] = star_rows[2] + k_at * res[2]
    res_out[...] = column([sigma] + star_rows + [k_at * res[1]])
    got = [
        send(res_out, res_in.at[0], below, 19), send(res_out, res_in.at[1], above, 20),
        send(res_out, res_in.at[2], near[-2], 21), send(res_out, res_in.at[3], near[2], 22),
        send(res_out, res_in.at[4], near[-3], 23), send(res_out, res_in.at[5], near[3], 20 + 15)]

    def spread(b, f):
        return down_x(b * up_x(f)) + down_y(b * up_y(f))

    qb = 0.25 * buoy
    qbl = 0.25 * b_low
    adj = scatter([res[3]], only, split3)
    gd = -adj * press[3]
    gk = scatter([-HALF * res[3] * div_at], only, split3)
    inj = [scatter([res[t]], only, split3) for t in range(steps - 1)]
    total = kappa * adj
    base = inj[2] + keep * adj + spread(qb, total) - (qb + qbl) * total
    for c in planes:
        c.wait_recv()
    k_near = [decode(k_in[i]) * (K_MAX / TOP) + K_MID for i in range(2)]
    d_near = [decode(d_in[i]) * (D_MAX / TOP) + D_MID for i in range(2)]
    k_near[0] = jnp.where(has_above, k_near[0], 0.0)
    b_near = [decode(b2_in[i]) * (B_MAX * 0.25 / TOP) + B_MID * 0.25 for i in range(2)]
    b_near[1] = jnp.where(slab > 1, b_near[1], 0.0)
    for c in got:
        c.wait_recv()

    def row(i, k):
        return res_in[i, k:k + 1]

    last, second, outer, first = [], [], [], []
    for i, d in enumerate((1, -1)):
        up, down = (fix_in[i, 0:1], fix_in[i, 3:4])
        up2, down2 = (fix2_in[i, 0:1], fix2_in[i, 3:4])
        out_row, in_row, out2, in2 = (up, down, up2, down2) if d > 0 else (down, up, down2, up2)
        last.append(scatter([row(i, 0)], [(d, 0, 0)], split2))
        first.append(scatter([row(i, 6)], [(d, 0, 0)], split2))
        second.append(scatter(
            [row(i, k) for k in range(1, 6)] + [out_row * row(i + 2, 0), in_row * sigma],
            spots(d, (2 * d, 0)), split2))
        rows_far = [row(i + 2, k) for k in range(1, 6)]
        rows_far[2] = rows_far[2] + row(i + 2, 0)
        outer.append(scatter(
            rows_far + [out2 * row(i + 4, 0), in2 * row(i, 0)],
            spots(2 * d, (3 * d, d)), split2))
    adj = base + qb * last[0] + qbl * last[1]
    gd = gd - adj * press[2]
    gk = gk - HALF * adj * divs[2]
    total = total + kappa * adj
    both = [last[i] + second[i] for i in range(2)]
    sa = first[0] + d_near[0] * second[0] + k_near[0] * (
        spread(b_near[0], both[0]) + b_near[0] * (outer[0] - both[0]) + qb * (total - both[0]))
    sb = first[1] + d_near[1] * second[1] + k_near[1] * (
        spread(qbl, both[1]) + qbl * (total - both[1]) + b_near[1] * (outer[1] - both[1]))
    adj = inj[1] + keep * adj + spread(qb, total) + (
        qb * (both[0] - total) + qbl * (both[1] - total))
    gd = gd - adj * press[1]
    gk = gk - HALF * adj * divs[1]
    total = total + kappa * adj
    adj = inj[0] + keep * adj + spread(qb, total) + (
        qb * (both[0] + sa - total) + qbl * (both[1] + sb - total))
    gd = gd - adj * press[0]
    gk = gk - HALF * adj * divs[0]
    gk = gk * (2.0 * dens[...] * speed[...])
    for i, g in enumerate((gk, gd)):
        grad[i] = g
        top = jnp.maximum(top_of(g), 1e-30)
        coded[i] = code_root(g, top)
        gscale[i] = jnp.broadcast_to(top * (1.0 / (TOP * TOP)), (8, 128))
    rows_out = 256 // n_grp
    copies = []
    for d in range(1, n_grp):
        peer = lax.rem(grp + d, n_grp)
        c = pltpu.make_async_remote_copy(
            src_ref=coded.at[:, pl.ds(pl.multiple_of(peer * rows_out, rows_out), rows_out)],
            dst_ref=gradrecv.at[d], send_sem=grad_send.at[d],
            recv_sem=grad_recv.at[d], device_id=(slab, peer), device_id_type=MESH)
        c.start()
        e = pltpu.make_async_remote_copy(
            src_ref=gscale, dst_ref=gscale_in.at[d], send_sem=gs_send.at[d],
            recv_sem=gs_recv.at[d], device_id=(slab, peer), device_id_type=MESH)
        e.start()
        copies.append((c, e))
    mine = pl.ds(pl.multiple_of(grp * rows_out, rows_out), rows_out)
    total = [grad[0, mine], grad[1, mine]]
    for d in range(1, n_grp):
        for c in copies[d - 1]:
            c.wait_recv()
        for i in range(2):
            total[i] = total[i] + decode_root(gradrecv[d, i]) * gscale_in[d, i, 0:1, 0:1]
    out_s[0] = total[0]
    out_a[0] = total[1]
    for c in pending + [c for pair in copies for c in pair]:
        c.wait_send()


def shards(
    n_slab, n_grp,
    sound_speed, density, attenuation, wavelet, weights, emitter_group, emitter_cell,
    receiver_cell, pressure_start, velocity_start, observed,
):
    vmem = pl.BlockSpec(memory_space=pltpu.VMEM)
    hbm = pl.BlockSpec(memory_space=pltpu.HBM)
    smem = pl.BlockSpec(memory_space=pltpu.SMEM)
    rows = 256 // n_grp
    plane = lambda *n, t=F32: pltpu.VMEM(n + (256, 256), t)
    tile = lambda *n: pltpu.VMEM(n + (8, 128), F32)
    out = jax.ShapeDtypeStruct((1, rows, 256), F32)
    dma = pltpu.SemaphoreType.DMA
    emit = weights.shape[1]
    return pl.pallas_call(
        functools.partial(kernel, n_slab, n_grp),
        out_shape=(out, out),
        in_specs=[smem] + [hbm] * 10,
        out_specs=(vmem, vmem),
        scratch_shapes=[
            plane(), plane(), plane(), plane(4), plane(3),
            pltpu.VMEM(weights.shape, BF16), pltpu.VMEM((1, emit), I32),
            pltpu.VMEM((1, emit), I32), pltpu.VMEM(observed.shape, BF16),
            pltpu.VMEM((7, 1, 128), I32),
            plane(t=I16), plane(t=I16), plane(t=I16), plane(t=I16),
            plane(t=I16), plane(t=I16), plane(t=I16), plane(2, t=I16),
            tile(), tile(2), tile(2), tile(2), tile(2), tile(2), tile(2), tile(2), tile(), tile(2),
            tile(), tile(6), tile(2), plane(t=I16), plane(2, t=I16), plane(t=I16),
            plane(2, t=I16), plane(2, t=I16),
            tile(n_grp), tile(n_grp), plane(2), plane(2, t=I16),
            pltpu.VMEM((n_grp, 2, rows, 256), I16), tile(2), tile(n_grp, 2),
            dma((10,)), dma((36,)), dma((36,)), dma((n_grp,)), dma((n_grp,)),
            dma((n_grp,)), dma((n_grp,)), dma((n_grp,)), dma((n_grp,)),
        ],
        compiler_params=pltpu.CompilerParams(
            collective_id=0, has_side_effects=True, vmem_limit_bytes=60 * 1024 * 1024),
    )(
        wavelet, sound_speed, density, attenuation, pressure_start, velocity_start, weights,
        emitter_group.reshape(1, -1), emitter_cell.reshape(1, -1),
        receiver_cell.reshape(1, -1), observed,
    )


def solution(mesh):
    return jax.shard_map(
        functools.partial(shards, mesh.shape["slab"], mesh.shape["grp"]),
        mesh=mesh,
        in_specs=(
            P("slab", None, None),
            P("slab", None, None),
            P("slab", None, None),
            P(),
            P(),
            P(),
            P(),
            P("slab"),
            P("grp", "slab", None, None),
            P(None, "grp", "slab", None, None),
            P("grp", None, "slab"),
        ),
        out_specs=(P("slab", "grp", None), P("slab", "grp", None)),
        check_vma=False,
    )
```

```python
import functools
import jax
import jax.numpy as jnp
from jax import lax
from jax.experimental import pallas as pl
from jax.experimental.pallas import tpu as pltpu
from jax.sharding import PartitionSpec as P

MESH = pl.DeviceIdType.MESH
HALF = 0.5
F32 = jnp.float32
BF16 = jnp.bfloat16


I16 = jnp.int16
I32 = jnp.int32
TOP = 32767.0
NT_DOT = (((1,), (1,)), ((), ()))


def split2(v):
    hi = v.astype(BF16)
    return hi, (v - hi.astype(F32)).astype(BF16)


def split3(v):
    hi = v.astype(BF16)
    rest = v - hi.astype(F32)
    mid = rest.astype(BF16)
    return hi, mid, (rest - mid.astype(F32)).astype(BF16)


def code(v):
    return jnp.round(v).astype(I32).astype(I16)


def decode(v):
    return v.astype(I32).astype(F32)


def code_root(v, top):
    root = jnp.sqrt(jnp.abs(v) * (1.0 / top)) * TOP
    return code(jnp.where(v < 0.0, -root, root))


def decode_root(v):
    u = decode(v)
    return u * jnp.abs(u)


def top_of(v):
    return jnp.max(jnp.max(jnp.abs(v), axis=0, keepdims=True), axis=1, keepdims=True)


P_MAX = 6.0
W_MAX = 7.3
V_MAX = 11.6
B_MID = 1.0714286
B_MAX = 0.3573
K_MID = 0.7875
K_MAX = 0.6127
D_MID = 0.895
D_MAX = 0.0952


def kernel(
    n_slab, n_grp,
    wav, speed_h, dens_h, atten_h, press_h, vel_h, weights_h, group_h, ecell_h, rcell_h, obs_h,
    out,
    speed, dens, atten, press, vel, weights, group, ecell, obs, rcs,
    p0_out, w_out, b_out, p1_out, p0_in, w_in, b_in, p1_in,
    p1_scale, p1_scale_in, p2_out, p2_in, far_out, far_in, part_out, part_in, fix_out, fix_in,
    res_out, res_in, fix2_in, k_out, k_in, d_out, d_in, b2_in,
    encsend, encrecv, grad, coded, gradrecv, gscale, gscale_in,
    load_sem, halo_send, halo_recv, enc_send, enc_recv, grad_send, grad_recv, gs_send, gs_recv,
):
    steps = 4
    slab = lax.axis_index("slab")
    grp = lax.axis_index("grp")
    above = lax.rem(slab + 1, n_slab)
    below = lax.rem(slab + n_slab - 1, n_slab)

    loads = [
        pltpu.make_async_copy(src, dst, load_sem.at[i])
        for i, (src, dst) in enumerate([
            (press_h.at[0, 0], press.at[0]), (dens_h.at[0], dens), (vel_h.at[:, 0, 0], vel),
            (rcell_h, rcs.at[3]), (weights_h, weights), (group_h, group), (obs_h, obs),
            (ecell_h, ecell), (speed_h.at[0], speed), (atten_h.at[0], atten),
        ])
    ]
    for c in loads:
        c.start()

    near = {d: lax.rem(slab + n_slab + d, n_slab) for d in (-3, -2, -1, 1, 2, 3)}
    barrier = pltpu.get_barrier_semaphore()
    for s in near.values():
        pl.semaphore_signal(barrier, inc=1, device_id=(s, grp), device_id_type=MESH)
    for d in range(1, n_grp):
        pl.semaphore_signal(
            barrier, inc=1, device_id=(slab, lax.rem(grp + d, n_grp)), device_id_type=MESH)

    for c in loads[:3]:
        c.wait()
    p0_out[...] = code(press[0] * (TOP / P_MAX))
    buoy = 1.0 / dens[...]
    w_out[...] = code((vel[0] + HALF * buoy * press[0]) * (TOP / W_MAX))
    b_out[...] = code((buoy - B_MID) * (TOP / B_MAX))
    loads[3].wait()
    pl.semaphore_wait(barrier, n_grp + 5)

    pending = []

    def send(src, dst, to, k):
        c = pltpu.make_async_remote_copy(
            src_ref=src, dst_ref=dst, send_sem=halo_send.at[k], recv_sem=halo_recv.at[k],
            device_id=(to, grp), device_id_type=MESH)
        c.start()
        pending.append(c)
        return c

    cells = [send(rcs.at[3], rcs.at[3 - d], near[d], 27 + d) for d in near]
    p0_down = send(p0_out, p0_in, below, 4)
    w_up = send(w_out, w_in, above, 5)
    b_up = send(b_out, b_in, above, 6)

    for c in loads[4:7]:
        c.wait()
    e_dev = obs.shape[0]
    eoff = pl.multiple_of(grp * e_dev, 128)
    wdev = weights[:, pl.ds(eoff, e_dev)].astype(F32)
    gdev = group[:, pl.ds(eoff, e_dev)]
    act_dev = jnp.where(
        gdev == lax.broadcasted_iota(I32, wdev.shape, 0), wdev, 0.0).astype(BF16)
    er = lax.broadcasted_iota(I32, (e_dev, e_dev * steps), 0)
    el = lax.broadcasted_iota(I32, (e_dev, e_dev * steps), 1)
    expand = jnp.where((el >> 2) == er, 1.0, 0.0).astype(BF16)
    wide = jnp.dot(act_dev, expand, preferred_element_type=F32).astype(BF16)
    rr = lax.broadcasted_iota(I32, (8 * n_grp, n_grp), 0)
    rl = lax.broadcasted_iota(I32, (8 * n_grp, n_grp), 1)
    rows = jnp.where((rr >> 3) == rl, 1.0, 0.0).astype(BF16)
    tall = jnp.dot(rows, wide, preferred_element_type=F32)
    tr = lax.broadcasted_iota(I32, tall.shape, 0)
    tl = lax.broadcasted_iota(I32, tall.shape, 1)
    lhs = jnp.where((tr & 7) == (tl & 3), tall, 0.0).astype(BF16)
    flat = obs[...].astype(F32).reshape(e_dev * steps, obs.shape[2]).astype(BF16)
    part = jnp.dot(lhs, flat, preferred_element_type=F32)
    encsend[...] = part.reshape(encsend.shape)
    enc_copies = []
    for d in range(1, n_grp):
        peer = lax.rem(grp + d, n_grp)
        c = pltpu.make_async_remote_copy(
            src_ref=encsend.at[peer], dst_ref=encrecv.at[d], send_sem=enc_send.at[d],
            recv_sem=enc_recv.at[d], device_id=(slab, peer), device_id_type=MESH)
        c.start()
        enc_copies.append(c)
    pending += enc_copies

    loads[7].wait()
    wall = weights[...].astype(F32)
    shot_row = lax.broadcasted_iota(I32, wall.shape, 0)
    own = jnp.sum(
        jnp.where((group[...] == shot_row) & (shot_row == grp), wall, 0.0),
        axis=0, keepdims=True)
    emit = wall.shape[1]
    ec = ecell[...] - slab * 65536
    ex = jnp.where((ec >= 0) & (ec < 65536), ec >> 8, -1)
    row_e = lax.broadcasted_iota(I32, (256, emit), 0)
    ax = jnp.where(row_e == ex, own, 0.0).astype(BF16)
    ay = jnp.where(row_e == (ec & 255), 1.0, 0.0).astype(BF16)
    amp = lax.dot_general(ax, ay, NT_DOT, preferred_element_type=F32)

    for c in cells:
        c.wait_recv()
    row_r = lax.broadcasted_iota(I32, (256, 128), 0)
    col_x, hot_y = {}, {}
    for d in range(-3, 4):
        rc = rcs[d + 3]
        inside = (slab + d >= 0) & (slab + d < n_slab)
        col_x[d] = jnp.where(inside, rc >> 8, -1000)
        y = jnp.where(inside, rc & 255, -1000)
        for dy in (-1, 0, 1) if abs(d) < 3 else (0,):
            hot_y[d, dy] = jnp.where(row_r == y + dy, 1.0, 0.0).astype(BF16)

    star = ((0, -1), (-1, 0), (0, 0), (1, 0), (0, 1))

    def spots(d, others):
        return [(d, dx, dy) for dx, dy in star] + [(o, 0, 0) for o in others]

    def blocks(points):
        return sorted({(d, dy) for d, _, dy in points})

    def gather(pieces, points):
        keys = blocks(points)
        wide = jnp.concatenate([hot_y[key] for key in keys], axis=1)
        values = jnp.dot(
            jnp.concatenate(pieces, axis=1), jnp.concatenate([wide] * len(pieces), axis=0),
            preferred_element_type=F32)
        table = {key: values[:, i * 128:(i + 1) * 128] for i, key in enumerate(keys)}
        return [
            jnp.sum(jnp.where(row_r == col_x[d] + dx, table[d, dy], 0.0), axis=0, keepdims=True)
            for d, dx, dy in points
        ]

    def scatter(values, points, split):
        left = []
        keys = blocks(points)
        for key in keys:
            total = 0.0
            for v, (d, dx, dy) in zip(values, points):
                if (d, dy) == key:
                    total = total + jnp.where(row_r == col_x[d] + dx, v, 0.0)
            left.append(total)
        right = [hot_y[key] for key in keys]
        pieces = [split(x) for x in left]
        count = len(pieces[0])
        lhs = jnp.concatenate([pc[i] for i in range(count) for pc in pieces], axis=1)
        rhs = jnp.concatenate(right * count, axis=1)
        return lax.dot_general(lhs, rhs, NT_DOT, preferred_element_type=F32)

    def column(rows_list):
        pad = 8 - len(rows_list)
        if pad:
            rows_list = rows_list + [jnp.zeros((pad, 128), F32)]
        return jnp.concatenate(rows_list, axis=0)

    only = [(0, 0, 0)]
    ring = spots(0, (1, -1))
    ones = jnp.ones((1, 128), F32)
    plain = lambda v: (v.astype(BF16),)
    count = scatter([ones] * 7, ring, plain)
    inv_ring = jnp.where(count > 0.5, 1.0 / count, 0.0)

    xi = lax.broadcasted_iota(I32, (256, 256), 0)
    yi = lax.broadcasted_iota(I32, (256, 256), 1)

    def up_x(f):
        return jnp.where(xi == 255, 0.0, pltpu.roll(f, 255, 0)) - f

    def up_y(f):
        return jnp.where(yi == 255, 0.0, pltpu.roll(f, 255, 1)) - f

    def down_x(f):
        return f - jnp.where(xi == 0, 0.0, pltpu.roll(f, 1, 0))

    def down_y(f):
        return f - jnp.where(yi == 0, 0.0, pltpu.roll(f, 1, 1))

    has_above = slab < n_slab - 1
    has_below = slab > 0
    for c in loads[8:]:
        c.wait()
    kappa = dens[...] * speed[...] * speed[...]
    keep = 1.0 - atten[...]
    hk = HALF * kappa
    hb = HALF * buoy

    def local_step(p, px, py):
        px = px - hb * up_x(p)
        py = py - hb * up_y(p)
        return px, py, down_x(px) + down_y(py)

    divs = [None] * steps
    recorded = [None] * steps
    p = press[0]
    px, py, flat_div = local_step(p, vel[1], vel[2])
    pz = vel[0] + hb * p
    base = keep * p + wav[0] * amp
    top = 1.001 * (
        top_of(base - hk * (pz + flat_div)) + P_MAX * top_of(hk * hb) + V_MAX * top_of(hk))
    p1_scale[...] = jnp.broadcast_to(top * (1.0 / TOP), (8, 128))
    got = [
        send(p1_scale, p1_scale_in.at[0], below, 9), send(p1_scale, p1_scale_in.at[1], above, 10)]
    to_code = TOP / top

    nearby = [(1, 0, 0), (-1, 0, 0)]
    kappa_at = gather(split2(kappa), spots(0, (1, -1)))
    buoy_at = gather(split2(buoy), [(0, 0, 0), (0, -1, 0), (0, 0, -1)] + nearby)
    keep_at = gather(split2(keep), only)[0]
    amp_at = gather(split2(amp), only)[0]

    p0_down.wait_recv()
    w_up.wait_recv()
    b_up.wait_recv()
    b_low = jnp.where(has_below, decode(b_in[...]) * (B_MAX / TOP) + B_MID, 0.0)
    hbl = HALF * b_low
    pzl = jnp.where(has_below, decode(w_in[...]) * (W_MAX / TOP), 0.0) - hbl * p
    pz = pz - hb * jnp.where(has_above, decode(p0_in[...]) * (P_MAX / TOP), 0.0)
    divs[0] = pz - pzl + flat_div
    p = base - hk * divs[0]
    press[1] = p

    p1_out[...] = code(p * to_code)
    got += [send(p1_out, p1_in.at[0], below, 7), send(p1_out, p1_in.at[1], above, 8)]

    k_out[...] = code((kappa - K_MID) * (TOP / K_MAX))
    d_out[...] = code((keep - D_MID) * (TOP / D_MAX))
    planes = [
        send(k_out, k_in.at[0], below, 0), send(k_out, k_in.at[1], above, 1),
        send(d_out, d_in.at[0], below, 2), send(d_out, d_in.at[1], above, 3)]
    low_at = gather(split2(b_low), only + nearby)
    fix_out[...] = column([
        0.25 * kappa_at[5] * buoy_at[3], 0.25 * kappa_at[5] * low_at[1],
        0.25 * kappa_at[6] * buoy_at[4], 0.25 * kappa_at[6] * low_at[2]])
    fixed = [
        send(fix_out, fix_in.at[0], below, 11), send(fix_out, fix_in.at[1], above, 12),
        send(fix_out, fix2_in.at[0], near[-2], 31), send(fix_out, fix2_in.at[1], near[2], 32)]
    k_at, b_at = kappa_at[2], buoy_at[0]
    own_at = 0.25 * k_at * b_at
    star_at = [
        kappa_at[0] * 0.25 * k_at * buoy_at[2],
        kappa_at[1] * 0.25 * k_at * buoy_at[1],
        k_at * (keep_at - 0.25 * k_at * (3.0 * b_at + buoy_at[1] + buoy_at[2] + low_at[0])),
        kappa_at[3] * own_at,
        kappa_at[4] * own_at]

    recorded[0] = gather(split2(p), only)[0]
    px, py, flat_div = local_step(p, px, py)
    pz = pz + hb * p
    pzl = pzl - hbl * p
    base = keep * p + wav[1] * amp
    for c in got:
        c.wait_recv()
    pz = pz - hb * jnp.where(has_above, decode(p1_in[0]) * p1_scale_in[0, 0:1, 0:1], 0.0)
    pzl = pzl + hbl * (decode(p1_in[1]) * p1_scale_in[1, 0:1, 0:1])
    divs[1] = pz - pzl + flat_div
    p = base - hk * divs[1]
    press[2] = p

    to_up, to_down = spots(1, (0, 2)), spots(-1, (0, -2))
    values = gather(split2(p), to_up + to_down)
    p2_out[0] = column(values[7:])
    p2_out[1] = column(values[:7])
    far_out[0] = column(values[13:])
    far_out[1] = column(values[6:7])
    got = [
        send(p2_out.at[0], p2_in.at[0], below, 13), send(p2_out.at[1], p2_in.at[1], above, 14)]
    far = [
        send(far_out.at[0], far_in.at[0], near[-2], 15),
        send(far_out.at[1], far_in.at[1], near[2], 16)]
    planes += [send(b_out, b2_in.at[0], below, 33), send(b_out, b2_in.at[1], near[2], 34)]
    px, py, flat_div = local_step(p, px, py)
    pz = pz + hb * p
    pzl = pzl - hbl * p
    flat_div = pz - pzl + flat_div
    base = keep * p + wav[2] * amp - hk * flat_div
    values = gather(split2(base), nearby)
    part_out[0] = column(values[1:])
    part_out[1] = column(values[:1])
    parts = [
        send(part_out.at[0], part_in.at[0], below, 17),
        send(part_out.at[1], part_in.at[1], above, 18)]
    recorded[1] = gather(split2(p), only)[0]
    for c in got:
        c.wait_recv()
    ua = hb * (inv_ring * scatter(
        [p2_in[0, i:i + 1] for i in range(7)], spots(0, (1, -1)), split2))
    ub = hbl * (inv_ring * scatter(
        [p2_in[1, i:i + 1] for i in range(7)], spots(0, (-1, 1)), split2))
    pz = pz - ua
    pzl = pzl + ub
    divs[2] = flat_div - ua - ub
    p = base + hk * (ua + ub)
    press[3] = p
    recorded[2] = gather(split2(p), only)[0]

    px, py, flat_div = local_step(p, px, py)
    div_at = gather(split2(pz + hb * p - (pzl - hbl * p) + flat_div), only)[0]
    for c in far + fixed + parts:
        c.wait_recv()
    pa = part_in[0, 0:1] + fix_in[0, 2:3] * far_in[0, 0:1] + fix_in[0, 3:4] * recorded[1]
    pb = part_in[1, 0:1] + fix_in[1, 0:1] * recorded[1] + fix_in[1, 1:2] * far_in[1, 0:1]
    pa = jnp.where(has_above, pa, 0.0)
    div_at = div_at - HALF * (b_at * pa + low_at[0] * pb)
    recorded[3] = keep_at * recorded[2] - HALF * k_at * div_at + wav[3] * amp_at

    for c in enc_copies:
        c.wait_recv()
    enc = encsend[grp]
    for d in range(1, n_grp):
        enc = enc + encrecv[d]
    res = [(recorded[t] - enc[t:t + 1]) * (1.0 / n_grp) for t in range(steps)]

    sigma = k_at * res[3]
    star_rows = [v * res[3] for v in star_at]
    star_rows[2] = star_rows[2] + k_at * res[2]
    res_out[...] = column([sigma] + star_rows + [k_at * res[1]])
    got = [
        send(res_out, res_in.at[0], below, 19), send(res_out, res_in.at[1], above, 20),
        send(res_out, res_in.at[2], near[-2], 21), send(res_out, res_in.at[3], near[2], 22),
        send(res_out, res_in.at[4], near[-3], 23), send(res_out, res_in.at[5], near[3], 20 + 15)]

    def spread(b, f):
        return down_x(b * up_x(f)) + down_y(b * up_y(f))

    qb = 0.25 * buoy
    qbl = 0.25 * b_low
    adj = scatter([res[3]], only, split3)
    gd = -adj * press[3]
    gk = scatter([-HALF * res[3] * div_at], only, split3)
    inj = [scatter([res[t]], only, split3) for t in range(steps - 1)]
    total = kappa * adj
    base = inj[2] + keep * adj + spread(qb, total) - (qb + qbl) * total
    for c in planes:
        c.wait_recv()
    k_near = [decode(k_in[i]) * (K_MAX / TOP) + K_MID for i in range(2)]
    d_near = [decode(d_in[i]) * (D_MAX / TOP) + D_MID for i in range(2)]
    k_near[0] = jnp.where(has_above, k_near[0], 0.0)
    b_near = [decode(b2_in[i]) * (B_MAX * 0.25 / TOP) + B_MID * 0.25 for i in range(2)]
    b_near[1] = jnp.where(slab > 1, b_near[1], 0.0)
    for c in got:
        c.wait_recv()

    def row(i, k):
        return res_in[i, k:k + 1]

    last, second, outer, first = [], [], [], []
    for i, d in enumerate((1, -1)):
        up, down = (fix_in[i, 0:1], fix_in[i, 3:4])
        up2, down2 = (fix2_in[i, 0:1], fix2_in[i, 3:4])
        out_row, in_row, out2, in2 = (up, down, up2, down2) if d > 0 else (down, up, down2, up2)
        last.append(scatter([row(i, 0)], [(d, 0, 0)], split2))
        first.append(scatter([row(i, 6)], [(d, 0, 0)], split2))
        second.append(scatter(
            [row(i, k) for k in range(1, 6)] + [out_row * row(i + 2, 0), in_row * sigma],
            spots(d, (2 * d, 0)), split2))
        rows_far = [row(i + 2, k) for k in range(1, 6)]
        rows_far[2] = rows_far[2] + row(i + 2, 0)
        outer.append(scatter(
            rows_far + [out2 * row(i + 4, 0), in2 * row(i, 0)],
            spots(2 * d, (3 * d, d)), split2))
    adj = base + qb * last[0] + qbl * last[1]
    gd = gd - adj * press[2]
    gk = gk - HALF * adj * divs[2]
    total = total + kappa * adj
    both = [last[i] + second[i] for i in range(2)]
    sa = first[0] + d_near[0] * second[0] + k_near[0] * (
        spread(b_near[0], both[0]) + b_near[0] * (outer[0] - both[0]) + qb * (total - both[0]))
    sb = first[1] + d_near[1] * second[1] + k_near[1] * (
        spread(qbl, both[1]) + qbl * (total - both[1]) + b_near[1] * (outer[1] - both[1]))
    adj = inj[1] + keep * adj + spread(qb, total) + (
        qb * (both[0] - total) + qbl * (both[1] - total))
    gd = gd - adj * press[1]
    gk = gk - HALF * adj * divs[1]
    total = total + kappa * adj
    adj = inj[0] + keep * adj + spread(qb, total) + (
        qb * (both[0] + sa - total) + qbl * (both[1] + sb - total))
    gd = gd - adj * press[0]
    gk = gk - HALF * adj * divs[0]
    gk = gk * (2.0 * dens[...] * speed[...])
    for i, g in enumerate((gk, gd)):
        grad[i] = g
        top = jnp.maximum(top_of(g), 1e-30)
        coded[i] = code_root(g, top)
        gscale[i] = jnp.broadcast_to(top * (1.0 / (TOP * TOP)), (8, 128))
    rows_out = 256 // n_grp
    copies = []
    for d in range(1, n_grp):
        peer = lax.rem(grp + d, n_grp)
        c = pltpu.make_async_remote_copy(
            src_ref=coded.at[:, pl.ds(pl.multiple_of(peer * rows_out, rows_out), rows_out)],
            dst_ref=gradrecv.at[d], send_sem=grad_send.at[d],
            recv_sem=grad_recv.at[d], device_id=(slab, peer), device_id_type=MESH)
        c.start()
        e = pltpu.make_async_remote_copy(
            src_ref=gscale, dst_ref=gscale_in.at[d], send_sem=gs_send.at[d],
            recv_sem=gs_recv.at[d], device_id=(slab, peer), device_id_type=MESH)
        e.start()
        copies.append((c, e))
    mine = pl.ds(pl.multiple_of(grp * rows_out, rows_out), rows_out)
    total = [grad[0, mine], grad[1, mine]]
    for d in range(1, n_grp):
        for c in copies[d - 1]:
            c.wait_recv()
        for i in range(2):
            total[i] = total[i] + decode_root(gradrecv[d, i]) * gscale_in[d, i, 0:1, 0:1]
    out[0] = total[0]
    out[1] = total[1]
    for c in pending + [c for pair in copies for c in pair]:
        c.wait_send()


def shards(
    n_slab, n_grp,
    sound_speed, density, attenuation, wavelet, weights, emitter_group, emitter_cell,
    receiver_cell, pressure_start, velocity_start, observed,
):
    vmem = pl.BlockSpec(memory_space=pltpu.VMEM)
    hbm = pl.BlockSpec(memory_space=pltpu.HBM)
    smem = pl.BlockSpec(memory_space=pltpu.SMEM)
    rows = 256 // n_grp
    plane = lambda *n, t=F32: pltpu.VMEM(n + (256, 256), t)
    tile = lambda *n: pltpu.VMEM(n + (8, 128), F32)
    out = jax.ShapeDtypeStruct((2, rows, 256), F32)
    dma = pltpu.SemaphoreType.DMA
    emit = weights.shape[1]
    both = pl.pallas_call(
        functools.partial(kernel, n_slab, n_grp),
        out_shape=out,
        in_specs=[smem] + [hbm] * 10,
        out_specs=vmem,
        scratch_shapes=[
            plane(), plane(), plane(), plane(4), plane(3),
            pltpu.VMEM(weights.shape, BF16), pltpu.VMEM((1, emit), I32),
            pltpu.VMEM((1, emit), I32), pltpu.VMEM(observed.shape, BF16),
            pltpu.VMEM((7, 1, 128), I32),
            plane(t=I16), plane(t=I16), plane(t=I16), plane(t=I16),
            plane(t=I16), plane(t=I16), plane(t=I16), plane(2, t=I16),
            tile(), tile(2), tile(2), tile(2), tile(2), tile(2), tile(2), tile(2), tile(), tile(2),
            tile(), tile(6), tile(2), plane(t=I16), plane(2, t=I16), plane(t=I16),
            plane(2, t=I16), plane(2, t=I16),
            tile(n_grp), tile(n_grp), plane(2), plane(2, t=I16),
            pltpu.VMEM((n_grp, 2, rows, 256), I16), tile(2), tile(n_grp, 2),
            dma((10,)), dma((36,)), dma((36,)), dma((n_grp,)), dma((n_grp,)),
            dma((n_grp,)), dma((n_grp,)), dma((n_grp,)), dma((n_grp,)),
        ],
        compiler_params=pltpu.CompilerParams(
            collective_id=0, has_side_effects=True, vmem_limit_bytes=60 * 1024 * 1024),
    )(
        wavelet, sound_speed, density, attenuation, pressure_start, velocity_start, weights,
        emitter_group.reshape(1, -1), emitter_cell.reshape(1, -1),
        receiver_cell.reshape(1, -1), observed,
    )
    return both[0:1], both[1:2]


def solution(mesh):
    return jax.shard_map(
        functools.partial(shards, mesh.shape["slab"], mesh.shape["grp"]),
        mesh=mesh,
        in_specs=(
            P("slab", None, None),
            P("slab", None, None),
            P("slab", None, None),
            P(),
            P(),
            P(),
            P(),
            P("slab"),
            P("grp", "slab", None, None),
            P(None, "grp", "slab", None, None),
            P("grp", None, "slab"),
        ),
        out_specs=(P("slab", "grp", None), P("slab", "grp", None)),
        check_vma=False,
    )
```

```python
import functools
import jax
import jax.numpy as jnp
from jax import lax
from jax.experimental import pallas as pl
from jax.experimental.pallas import tpu as pltpu
from jax.sharding import PartitionSpec as P

MESH = pl.DeviceIdType.MESH
HALF = 0.5
F32 = jnp.float32
BF16 = jnp.bfloat16


I16 = jnp.int16
I32 = jnp.int32
TOP = 32767.0
NT_DOT = (((1,), (1,)), ((), ()))


def split2(v):
    hi = v.astype(BF16)
    return hi, (v - hi.astype(F32)).astype(BF16)


def split3(v):
    hi = v.astype(BF16)
    rest = v - hi.astype(F32)
    mid = rest.astype(BF16)
    return hi, mid, (rest - mid.astype(F32)).astype(BF16)


def code(v):
    return jnp.round(v).astype(I32).astype(I16)


def decode(v):
    return v.astype(I32).astype(F32)


def code_root(v, top):
    root = jnp.sqrt(jnp.abs(v) * (1.0 / top)) * TOP
    return code(jnp.where(v < 0.0, -root, root))


def decode_root(v):
    u = decode(v)
    return u * jnp.abs(u)


def top_of(v):
    return jnp.max(jnp.max(jnp.abs(v), axis=0, keepdims=True), axis=1, keepdims=True)


P_MAX = 6.0
W_MAX = 7.3
V_MAX = 11.6
B_MID = 1.0714286
B_MAX = 0.3573
K_MID = 0.7875
K_MAX = 0.6127
D_MID = 0.895
D_MAX = 0.0952


def kernel(
    n_slab, n_grp,
    wav, speed_h, dens_h, atten_h, press_h, vel_h, weights_h, group_h, ecell_h, rcell_h, obs_h,
    out,
    speed, dens, atten, press, vel, weights, group, ecell, obs, rcs,
    p0_out, w_out, p1_out, p0_in, w_in, b_in, p1_in,
    p1_scale, p1_scale_in, p2_out, p2_in, far_out, far_in, part_out, part_in, fix_out, fix_in,
    res_out, res_in, fix2_in, near_out, near_in,
    encsend, encrecv, grad, coded, gradrecv, gscale, gscale_in,
    load_sem, halo_send, halo_recv, enc_send, enc_recv, grad_send, grad_recv, gs_send, gs_recv,
):
    steps = 4
    slab = lax.axis_index("slab")
    grp = lax.axis_index("grp")
    above = lax.rem(slab + 1, n_slab)
    below = lax.rem(slab + n_slab - 1, n_slab)

    loads = [
        pltpu.make_async_copy(src, dst, load_sem.at[i])
        for i, (src, dst) in enumerate([
            (press_h.at[0, 0], press.at[0]), (dens_h.at[0], dens), (vel_h.at[:, 0, 0], vel),
            (rcell_h, rcs.at[3]), (weights_h, weights), (group_h, group), (obs_h, obs),
            (ecell_h, ecell), (speed_h.at[0], speed), (atten_h.at[0], atten),
        ])
    ]
    for c in loads:
        c.start()

    near = {d: lax.rem(slab + n_slab + d, n_slab) for d in (-3, -2, -1, 1, 2, 3)}
    barrier = pltpu.get_barrier_semaphore()
    for s in near.values():
        pl.semaphore_signal(barrier, inc=1, device_id=(s, grp), device_id_type=MESH)
    for d in range(1, n_grp):
        pl.semaphore_signal(
            barrier, inc=1, device_id=(slab, lax.rem(grp + d, n_grp)), device_id_type=MESH)

    for c in loads[:3]:
        c.wait()
    p0_out[...] = code(press[0] * (TOP / P_MAX))
    buoy = 1.0 / dens[...]
    w_out[...] = code((vel[0] + HALF * buoy * press[0]) * (TOP / W_MAX))
    near_out[2] = code((buoy - B_MID) * (TOP / B_MAX))
    for c in loads[4:7]:
        c.wait()
    e_dev = obs.shape[0]
    eoff = pl.multiple_of(grp * e_dev, 128)
    wdev = weights[:, pl.ds(eoff, e_dev)].astype(F32)
    gdev = group[:, pl.ds(eoff, e_dev)]
    act_dev = jnp.where(
        gdev == lax.broadcasted_iota(I32, wdev.shape, 0), wdev, 0.0).astype(BF16)
    er = lax.broadcasted_iota(I32, (e_dev, e_dev * steps), 0)
    el = lax.broadcasted_iota(I32, (e_dev, e_dev * steps), 1)
    expand = jnp.where((el >> 2) == er, 1.0, 0.0).astype(BF16)
    wide = jnp.dot(act_dev, expand, preferred_element_type=F32).astype(BF16)
    rr = lax.broadcasted_iota(I32, (8 * n_grp, n_grp), 0)
    rl = lax.broadcasted_iota(I32, (8 * n_grp, n_grp), 1)
    rows = jnp.where((rr >> 3) == rl, 1.0, 0.0).astype(BF16)
    tall = jnp.dot(rows, wide, preferred_element_type=F32)
    tr = lax.broadcasted_iota(I32, tall.shape, 0)
    tl = lax.broadcasted_iota(I32, tall.shape, 1)
    lhs = jnp.where((tr & 7) == (tl & 3), tall, 0.0).astype(BF16)
    flat = obs[...].astype(F32).reshape(e_dev * steps, obs.shape[2]).astype(BF16)
    part = jnp.dot(lhs, flat, preferred_element_type=F32)
    encsend[...] = part.reshape(encsend.shape)
    loads[7].wait()
    wall = weights[...].astype(F32)
    shot_row = lax.broadcasted_iota(I32, wall.shape, 0)
    own = jnp.sum(
        jnp.where((group[...] == shot_row) & (shot_row == grp), wall, 0.0),
        axis=0, keepdims=True)
    emit = wall.shape[1]
    ec = ecell[...] - slab * 65536
    ex = jnp.where((ec >= 0) & (ec < 65536), ec >> 8, -1)
    row_e = lax.broadcasted_iota(I32, (256, emit), 0)
    ax = jnp.where(row_e == ex, own, 0.0).astype(BF16)
    ay = jnp.where(row_e == (ec & 255), 1.0, 0.0).astype(BF16)
    amp = lax.dot_general(ax, ay, NT_DOT, preferred_element_type=F32)

    xi = lax.broadcasted_iota(I32, (256, 256), 0)
    yi = lax.broadcasted_iota(I32, (256, 256), 1)

    def up_x(f):
        return jnp.where(xi == 255, 0.0, pltpu.roll(f, 255, 0)) - f

    def up_y(f):
        return jnp.where(yi == 255, 0.0, pltpu.roll(f, 255, 1)) - f

    def down_x(f):
        return f - jnp.where(xi == 0, 0.0, pltpu.roll(f, 1, 0))

    def down_y(f):
        return f - jnp.where(yi == 0, 0.0, pltpu.roll(f, 1, 1))

    has_above = slab < n_slab - 1
    has_below = slab > 0
    for c in loads[8:]:
        c.wait()
    kappa = dens[...] * speed[...] * speed[...]
    keep = 1.0 - atten[...]
    near_out[0] = code((kappa - K_MID) * (TOP / K_MAX))
    near_out[1] = code((keep - D_MID) * (TOP / D_MAX))
    hk = HALF * kappa
    hb = HALF * buoy

    def local_step(p, px, py):
        px = px - hb * up_x(p)
        py = py - hb * up_y(p)
        return px, py, down_x(px) + down_y(py)

    divs = [None] * steps
    recorded = [None] * steps
    p = press[0]
    px, py, flat_div = local_step(p, vel[1], vel[2])
    pz = vel[0] + hb * p
    base = keep * p + wav[0] * amp
    top = 1.001 * (
        top_of(base - hk * (pz + flat_div)) + P_MAX * top_of(hk * hb) + V_MAX * top_of(hk))
    p1_scale[...] = jnp.broadcast_to(top * (1.0 / TOP), (8, 128))
    loads[3].wait()
    pl.semaphore_wait(barrier, n_grp + 5)

    pending = []

    def send(src, dst, to, k):
        c = pltpu.make_async_remote_copy(
            src_ref=src, dst_ref=dst, send_sem=halo_send.at[k], recv_sem=halo_recv.at[k],
            device_id=(to, grp), device_id_type=MESH)
        c.start()
        pending.append(c)
        return c

    cells = [send(rcs.at[3], rcs.at[3 - d], near[d], 27 + d) for d in near]
    p0_down = send(p0_out, p0_in, below, 4)
    w_up = send(w_out, w_in, above, 5)
    b_up = send(near_out.at[2], b_in, above, 6)
    quarter = pl.ds(pl.multiple_of(lax.rem(grp, 4) * 64, 64), 64)
    pieces_in = [
        send(near_out.at[:, quarter], near_in.at[0, :, quarter], below, 0),
        send(near_out.at[0:2, quarter], near_in.at[1, 0:2, quarter], above, 1),
        send(near_out.at[2, quarter], near_in.at[1, 2, quarter], near[2], 33)]

    enc_copies = []
    for d in range(1, n_grp):
        peer = lax.rem(grp + d, n_grp)
        c = pltpu.make_async_remote_copy(
            src_ref=encsend.at[peer], dst_ref=encrecv.at[d], send_sem=enc_send.at[d],
            recv_sem=enc_recv.at[d], device_id=(slab, peer), device_id_type=MESH)
        c.start()
        enc_copies.append(c)
    pending += enc_copies

    for c in cells:
        c.wait_recv()
    row_r = lax.broadcasted_iota(I32, (256, 128), 0)
    col_x, hot_y = {}, {}
    for d in range(-3, 4):
        rc = rcs[d + 3]
        inside = (slab + d >= 0) & (slab + d < n_slab)
        col_x[d] = jnp.where(inside, rc >> 8, -1000)
        y = jnp.where(inside, rc & 255, -1000)
        for dy in (-1, 0, 1) if abs(d) < 3 else (0,):
            hot_y[d, dy] = jnp.where(row_r == y + dy, 1.0, 0.0).astype(BF16)

    star = ((0, -1), (-1, 0), (0, 0), (1, 0), (0, 1))

    def spots(d, others):
        return [(d, dx, dy) for dx, dy in star] + [(o, 0, 0) for o in others]

    def blocks(points):
        return sorted({(d, dy) for d, _, dy in points})

    def gather(pieces, points):
        keys = blocks(points)
        wide = jnp.concatenate([hot_y[key] for key in keys], axis=1)
        values = jnp.dot(
            jnp.concatenate(pieces, axis=1), jnp.concatenate([wide] * len(pieces), axis=0),
            preferred_element_type=F32)
        table = {key: values[:, i * 128:(i + 1) * 128] for i, key in enumerate(keys)}
        return [
            jnp.sum(jnp.where(row_r == col_x[d] + dx, table[d, dy], 0.0), axis=0, keepdims=True)
            for d, dx, dy in points
        ]

    def scatter(values, points, split):
        left = []
        keys = blocks(points)
        for key in keys:
            total = 0.0
            for v, (d, dx, dy) in zip(values, points):
                if (d, dy) == key:
                    total = total + jnp.where(row_r == col_x[d] + dx, v, 0.0)
            left.append(total)
        right = [hot_y[key] for key in keys]
        pieces = [split(x) for x in left]
        count = len(pieces[0])
        lhs = jnp.concatenate([pc[i] for i in range(count) for pc in pieces], axis=1)
        rhs = jnp.concatenate(right * count, axis=1)
        return lax.dot_general(lhs, rhs, NT_DOT, preferred_element_type=F32)

    def column(rows_list):
        pad = 8 - len(rows_list)
        if pad:
            rows_list = rows_list + [jnp.zeros((pad, 128), F32)]
        return jnp.concatenate(rows_list, axis=0)

    only = [(0, 0, 0)]
    ring = spots(0, (1, -1))
    ones = jnp.ones((1, 128), F32)
    plain = lambda v: (v.astype(BF16),)
    count = scatter([ones] * 7, ring, plain)
    inv_ring = jnp.where(count > 0.5, 1.0 / count, 0.0)

    got = [
        send(p1_scale, p1_scale_in.at[0], below, 9), send(p1_scale, p1_scale_in.at[1], above, 10)]
    to_code = TOP / top

    nearby = [(1, 0, 0), (-1, 0, 0)]
    kappa_at = gather(split2(kappa), spots(0, (1, -1)))
    buoy_at = gather(split2(buoy), [(0, 0, 0), (0, -1, 0), (0, 0, -1)] + nearby)
    keep_at = gather(split2(keep), only)[0]
    amp_at = gather(split2(amp), only)[0]

    p0_down.wait_recv()
    w_up.wait_recv()
    b_up.wait_recv()
    b_low = jnp.where(has_below, decode(b_in[...]) * (B_MAX / TOP) + B_MID, 0.0)
    hbl = HALF * b_low
    pzl = jnp.where(has_below, decode(w_in[...]) * (W_MAX / TOP), 0.0) - hbl * p
    pz = pz - hb * jnp.where(has_above, decode(p0_in[...]) * (P_MAX / TOP), 0.0)
    divs[0] = pz - pzl + flat_div
    p = base - hk * divs[0]
    press[1] = p

    p1_out[...] = code(p * to_code)
    got += [send(p1_out, p1_in.at[0], below, 7), send(p1_out, p1_in.at[1], above, 8)]

    low_at = gather(split2(b_low), only + nearby)
    fix_out[...] = column([
        0.25 * kappa_at[5] * buoy_at[3], 0.25 * kappa_at[5] * low_at[1],
        0.25 * kappa_at[6] * buoy_at[4], 0.25 * kappa_at[6] * low_at[2]])
    fixed = [
        send(fix_out, fix_in.at[0], below, 11), send(fix_out, fix_in.at[1], above, 12),
        send(fix_out, fix2_in.at[0], near[-2], 31), send(fix_out, fix2_in.at[1], near[2], 32)]
    for c in pieces_in:
        c.wait_recv()
    planes = []
    for d in range(1, 4):
        c = pltpu.make_async_remote_copy(
            src_ref=near_in.at[:, :, quarter], dst_ref=near_in.at[:, :, quarter],
            send_sem=halo_send.at[(2, 3, 34)[d - 1]], recv_sem=halo_recv.at[(2, 3, 34)[d - 1]],
            device_id=(slab, lax.div(grp, 4) * 4 + lax.rem(lax.rem(grp, 4) + d, 4)),
            device_id_type=MESH)
        c.start()
        planes.append(c)
    pending += planes
    k_at, b_at = kappa_at[2], buoy_at[0]
    own_at = 0.25 * k_at * b_at
    star_at = [
        kappa_at[0] * 0.25 * k_at * buoy_at[2],
        kappa_at[1] * 0.25 * k_at * buoy_at[1],
        k_at * (keep_at - 0.25 * k_at * (3.0 * b_at + buoy_at[1] + buoy_at[2] + low_at[0])),
        kappa_at[3] * own_at,
        kappa_at[4] * own_at]

    recorded[0] = gather(split2(p), only)[0]
    px, py, flat_div = local_step(p, px, py)
    pz = pz + hb * p
    pzl = pzl - hbl * p
    base = keep * p + wav[1] * amp
    for c in got:
        c.wait_recv()
    pz = pz - hb * jnp.where(has_above, decode(p1_in[0]) * p1_scale_in[0, 0:1, 0:1], 0.0)
    pzl = pzl + hbl * (decode(p1_in[1]) * p1_scale_in[1, 0:1, 0:1])
    divs[1] = pz - pzl + flat_div
    p = base - hk * divs[1]
    press[2] = p

    to_up, to_down = spots(1, (0, 2)), spots(-1, (0, -2))
    values = gather(split2(p), to_up + to_down)
    p2_out[0] = column(values[7:])
    p2_out[1] = column(values[:7])
    far_out[0] = column(values[13:])
    far_out[1] = column(values[6:7])
    got = [
        send(p2_out.at[0], p2_in.at[0], below, 13), send(p2_out.at[1], p2_in.at[1], above, 14)]
    far = [
        send(far_out.at[0], far_in.at[0], near[-2], 15),
        send(far_out.at[1], far_in.at[1], near[2], 16)]
    px, py, flat_div = local_step(p, px, py)
    pz = pz + hb * p
    pzl = pzl - hbl * p
    flat_div = pz - pzl + flat_div
    base = keep * p + wav[2] * amp - hk * flat_div
    values = gather(split2(base), nearby)
    part_out[0] = column(values[1:])
    part_out[1] = column(values[:1])
    parts = [
        send(part_out.at[0], part_in.at[0], below, 17),
        send(part_out.at[1], part_in.at[1], above, 18)]
    recorded[1] = gather(split2(p), only)[0]
    for c in got:
        c.wait_recv()
    ua = hb * (inv_ring * scatter(
        [p2_in[0, i:i + 1] for i in range(7)], spots(0, (1, -1)), split2))
    ub = hbl * (inv_ring * scatter(
        [p2_in[1, i:i + 1] for i in range(7)], spots(0, (-1, 1)), split2))
    pz = pz - ua
    pzl = pzl + ub
    divs[2] = flat_div - ua - ub
    p = base + hk * (ua + ub)
    press[3] = p
    recorded[2] = gather(split2(p), only)[0]

    px, py, flat_div = local_step(p, px, py)
    div_at = gather(split2(pz + hb * p - (pzl - hbl * p) + flat_div), only)[0]
    for c in far + fixed + parts:
        c.wait_recv()
    pa = part_in[0, 0:1] + fix_in[0, 2:3] * far_in[0, 0:1] + fix_in[0, 3:4] * recorded[1]
    pb = part_in[1, 0:1] + fix_in[1, 0:1] * recorded[1] + fix_in[1, 1:2] * far_in[1, 0:1]
    pa = jnp.where(has_above, pa, 0.0)
    div_at = div_at - HALF * (b_at * pa + low_at[0] * pb)
    recorded[3] = keep_at * recorded[2] - HALF * k_at * div_at + wav[3] * amp_at

    for c in enc_copies:
        c.wait_recv()
    enc = encsend[grp]
    for d in range(1, n_grp):
        enc = enc + encrecv[d]
    res = [(recorded[t] - enc[t:t + 1]) * (1.0 / n_grp) for t in range(steps)]

    sigma = k_at * res[3]
    star_rows = [v * res[3] for v in star_at]
    star_rows[2] = star_rows[2] + k_at * res[2]
    res_out[...] = column([sigma] + star_rows + [k_at * res[1]])
    got = [
        send(res_out, res_in.at[0], below, 19), send(res_out, res_in.at[1], above, 20),
        send(res_out, res_in.at[2], near[-2], 21), send(res_out, res_in.at[3], near[2], 22),
        send(res_out, res_in.at[4], near[-3], 23), send(res_out, res_in.at[5], near[3], 20 + 15)]

    def spread(b, f):
        return down_x(b * up_x(f)) + down_y(b * up_y(f))

    qb = 0.25 * buoy
    qbl = 0.25 * b_low
    adj = scatter([res[3]], only, split3)
    gd = -adj * press[3]
    gk = scatter([-HALF * res[3] * div_at], only, split3)
    inj = [scatter([res[t]], only, split3) for t in range(steps - 1)]
    total = kappa * adj
    base = inj[2] + keep * adj + spread(qb, total) - (qb + qbl) * total
    for c in planes:
        c.wait_recv()
    k_near = [decode(near_in[i, 0]) * (K_MAX / TOP) + K_MID for i in range(2)]
    d_near = [decode(near_in[i, 1]) * (D_MAX / TOP) + D_MID for i in range(2)]
    k_near[0] = jnp.where(has_above, k_near[0], 0.0)
    b_near = [decode(near_in[i, 2]) * (B_MAX * 0.25 / TOP) + B_MID * 0.25 for i in range(2)]
    b_near[1] = jnp.where(slab > 1, b_near[1], 0.0)
    for c in got:
        c.wait_recv()

    def row(i, k):
        return res_in[i, k:k + 1]

    last, second, outer, first = [], [], [], []
    for i, d in enumerate((1, -1)):
        up, down = (fix_in[i, 0:1], fix_in[i, 3:4])
        up2, down2 = (fix2_in[i, 0:1], fix2_in[i, 3:4])
        out_row, in_row, out2, in2 = (up, down, up2, down2) if d > 0 else (down, up, down2, up2)
        last.append(scatter([row(i, 0)], [(d, 0, 0)], split2))
        first.append(scatter([row(i, 6)], [(d, 0, 0)], split2))
        second.append(scatter(
            [row(i, k) for k in range(1, 6)] + [out_row * row(i + 2, 0), in_row * sigma],
            spots(d, (2 * d, 0)), split2))
        rows_far = [row(i + 2, k) for k in range(1, 6)]
        rows_far[2] = rows_far[2] + row(i + 2, 0)
        outer.append(scatter(
            rows_far + [out2 * row(i + 4, 0), in2 * row(i, 0)],
            spots(2 * d, (3 * d, d)), split2))
    adj = base + qb * last[0] + qbl * last[1]
    gd = gd - adj * press[2]
    gk = gk - HALF * adj * divs[2]
    total = total + kappa * adj
    both = [last[i] + second[i] for i in range(2)]
    sa = first[0] + d_near[0] * second[0] + k_near[0] * (
        spread(b_near[0], both[0]) + b_near[0] * (outer[0] - both[0]) + qb * (total - both[0]))
    sb = first[1] + d_near[1] * second[1] + k_near[1] * (
        spread(qbl, both[1]) + qbl * (total - both[1]) + b_near[1] * (outer[1] - both[1]))
    adj = inj[1] + keep * adj + spread(qb, total) + (
        qb * (both[0] - total) + qbl * (both[1] - total))
    gd = gd - adj * press[1]
    gk = gk - HALF * adj * divs[1]
    total = total + kappa * adj
    adj = inj[0] + keep * adj + spread(qb, total) + (
        qb * (both[0] + sa - total) + qbl * (both[1] + sb - total))
    gd = gd - adj * press[0]
    gk = gk - HALF * adj * divs[0]
    gk = gk * (2.0 * dens[...] * speed[...])
    for i, g in enumerate((gk, gd)):
        grad[i] = g
        top = jnp.maximum(top_of(g), 1e-30)
        coded[i] = code_root(g, top)
        gscale[i] = jnp.broadcast_to(top * (1.0 / (TOP * TOP)), (8, 128))
    rows_out = 256 // n_grp
    copies = []
    for d in range(1, n_grp):
        peer = lax.rem(grp + d, n_grp)
        c = pltpu.make_async_remote_copy(
            src_ref=coded.at[:, pl.ds(pl.multiple_of(peer * rows_out, rows_out), rows_out)],
            dst_ref=gradrecv.at[d], send_sem=grad_send.at[d],
            recv_sem=grad_recv.at[d], device_id=(slab, peer), device_id_type=MESH)
        c.start()
        e = pltpu.make_async_remote_copy(
            src_ref=gscale, dst_ref=gscale_in.at[d], send_sem=gs_send.at[d],
            recv_sem=gs_recv.at[d], device_id=(slab, peer), device_id_type=MESH)
        e.start()
        copies.append((c, e))
    mine = pl.ds(pl.multiple_of(grp * rows_out, rows_out), rows_out)
    total = [grad[0, mine], grad[1, mine]]
    for d in range(1, n_grp):
        for c in copies[d - 1]:
            c.wait_recv()
        for i in range(2):
            total[i] = total[i] + decode_root(gradrecv[d, i]) * gscale_in[d, i, 0:1, 0:1]
    out[0] = total[0]
    out[1] = total[1]
    for c in pending + [c for pair in copies for c in pair]:
        c.wait_send()


def shards(
    n_slab, n_grp,
    sound_speed, density, attenuation, wavelet, weights, emitter_group, emitter_cell,
    receiver_cell, pressure_start, velocity_start, observed,
):
    vmem = pl.BlockSpec(memory_space=pltpu.VMEM)
    hbm = pl.BlockSpec(memory_space=pltpu.HBM)
    smem = pl.BlockSpec(memory_space=pltpu.SMEM)
    rows = 256 // n_grp
    plane = lambda *n, t=F32: pltpu.VMEM(n + (256, 256), t)
    tile = lambda *n: pltpu.VMEM(n + (8, 128), F32)
    out = jax.ShapeDtypeStruct((2, rows, 256), F32)
    dma = pltpu.SemaphoreType.DMA
    emit = weights.shape[1]
    both = pl.pallas_call(
        functools.partial(kernel, n_slab, n_grp),
        out_shape=out,
        in_specs=[smem] + [hbm] * 10,
        out_specs=vmem,
        scratch_shapes=[
            plane(), plane(), plane(), plane(4), plane(3),
            pltpu.VMEM(weights.shape, BF16), pltpu.VMEM((1, emit), I32),
            pltpu.VMEM((1, emit), I32), pltpu.VMEM(observed.shape, BF16),
            pltpu.VMEM((7, 1, 128), I32),
            plane(t=I16), plane(t=I16), plane(t=I16),
            plane(t=I16), plane(t=I16), plane(t=I16), plane(2, t=I16),
            tile(), tile(2), tile(2), tile(2), tile(2), tile(2), tile(2), tile(2), tile(), tile(2),
            tile(), tile(6), tile(2), plane(3, t=I16), plane(2, 3, t=I16),
            tile(n_grp), tile(n_grp), plane(2), plane(2, t=I16),
            pltpu.VMEM((n_grp, 2, rows, 256), I16), tile(2), tile(n_grp, 2),
            dma((10,)), dma((36,)), dma((36,)), dma((n_grp,)), dma((n_grp,)),
            dma((n_grp,)), dma((n_grp,)), dma((n_grp,)), dma((n_grp,)),
        ],
        compiler_params=pltpu.CompilerParams(
            collective_id=0, has_side_effects=True, vmem_limit_bytes=60 * 1024 * 1024),
    )(
        wavelet, sound_speed, density, attenuation, pressure_start, velocity_start, weights,
        emitter_group.reshape(1, -1), emitter_cell.reshape(1, -1),
        receiver_cell.reshape(1, -1), observed,
    )
    return both[0:1], both[1:2]


def solution(mesh):
    return jax.shard_map(
        functools.partial(shards, mesh.shape["slab"], mesh.shape["grp"]),
        mesh=mesh,
        in_specs=(
            P("slab", None, None),
            P("slab", None, None),
            P("slab", None, None),
            P(),
            P(),
            P(),
            P(),
            P("slab"),
            P("grp", "slab", None, None),
            P(None, "grp", "slab", None, None),
            P("grp", None, "slab"),
        ),
        out_specs=(P("slab", "grp", None), P("slab", "grp", None)),
        check_vma=False,
    )
```

```python
import functools
import jax
import jax.numpy as jnp
from jax import lax
from jax.experimental import pallas as pl
from jax.experimental.pallas import tpu as pltpu
from jax.sharding import PartitionSpec as P

MESH = pl.DeviceIdType.MESH
HALF = 0.5
F32 = jnp.float32
BF16 = jnp.bfloat16


I16 = jnp.int16
I32 = jnp.int32
TOP = 32767.0
NT_DOT = (((1,), (1,)), ((), ()))


def split2(v):
    hi = v.astype(BF16)
    return hi, (v - hi.astype(F32)).astype(BF16)


def split3(v):
    hi = v.astype(BF16)
    rest = v - hi.astype(F32)
    mid = rest.astype(BF16)
    return hi, mid, (rest - mid.astype(F32)).astype(BF16)


def code(v):
    return jnp.round(v).astype(I32).astype(I16)


def decode(v):
    return v.astype(I32).astype(F32)


def code_root(v, top):
    root = jnp.sqrt(jnp.abs(v) * (1.0 / top)) * TOP
    return code(jnp.where(v < 0.0, -root, root))


def decode_root(v):
    u = decode(v)
    return u * jnp.abs(u)


def top_of(v):
    return jnp.max(jnp.max(jnp.abs(v), axis=0, keepdims=True), axis=1, keepdims=True)


P_MAX = 6.0
W_MAX = 7.3
V_MAX = 11.6
B_MID = 1.0714286
B_MAX = 0.3573
K_MID = 0.7875
K_MAX = 0.6127
D_MID = 0.895
D_MAX = 0.0952


def kernel(
    n_slab, n_grp,
    wav, speed_h, dens_h, atten_h, press_h, vel_h, weights_h, group_h, ecell_h, rcell_h, obs_h,
    out,
    speed, dens, atten, press, vel, weights, group, ecell, obs, rcs,
    p0_out, w_out, p1_out, p0_in, w_in, b_in, p1_in,
    p1_scale, p1_scale_in, p2_out, p2_in, far_out, far_in, part_out, part_in, fix_out, fix_in,
    res_out, res_in, fix2_in, near_out, near_in,
    encsend, encrecv, grad, coded, gradrecv, gscale, gscale_in,
    load_sem, halo_send, halo_recv, enc_send, enc_recv, grad_send, grad_recv, gs_send, gs_recv,
):
    steps = 4
    slab = lax.axis_index("slab")
    grp = lax.axis_index("grp")
    above = lax.rem(slab + 1, n_slab)
    below = lax.rem(slab + n_slab - 1, n_slab)

    loads = [
        pltpu.make_async_copy(src, dst, load_sem.at[i])
        for i, (src, dst) in enumerate([
            (press_h.at[0, 0], press.at[0]), (dens_h.at[0], dens), (vel_h.at[:, 0, 0], vel),
            (rcell_h, rcs.at[3]), (weights_h, weights), (group_h, group), (obs_h, obs),
            (ecell_h, ecell), (speed_h.at[0], speed), (atten_h.at[0], atten),
        ])
    ]
    for c in loads:
        c.start()

    near = {d: lax.rem(slab + n_slab + d, n_slab) for d in (-3, -2, -1, 1, 2, 3)}
    barrier = pltpu.get_barrier_semaphore()
    for s in near.values():
        pl.semaphore_signal(barrier, inc=1, device_id=(s, grp), device_id_type=MESH)
    for d in range(1, n_grp):
        pl.semaphore_signal(
            barrier, inc=1, device_id=(slab, lax.rem(grp + d, n_grp)), device_id_type=MESH)

    for c in loads[:3]:
        c.wait()
    p0_out[...] = code(press[0] * (TOP / P_MAX))
    buoy = 1.0 / dens[...]
    w_out[...] = code((vel[0] + HALF * buoy * press[0]) * (TOP / W_MAX))
    near_out[2] = code((buoy - B_MID) * (TOP / B_MAX))
    for c in loads[4:7]:
        c.wait()
    e_dev = obs.shape[0]
    eoff = pl.multiple_of(grp * e_dev, 128)
    wdev = weights[:, pl.ds(eoff, e_dev)].astype(F32)
    gdev = group[:, pl.ds(eoff, e_dev)]
    act_dev = jnp.where(
        gdev == lax.broadcasted_iota(I32, wdev.shape, 0), wdev, 0.0).astype(BF16)
    er = lax.broadcasted_iota(I32, (e_dev, e_dev * steps), 0)
    el = lax.broadcasted_iota(I32, (e_dev, e_dev * steps), 1)
    expand = jnp.where((el >> 2) == er, 1.0, 0.0).astype(BF16)
    wide = jnp.dot(act_dev, expand, preferred_element_type=F32).astype(BF16)
    rr = lax.broadcasted_iota(I32, (8 * n_grp, n_grp), 0)
    rl = lax.broadcasted_iota(I32, (8 * n_grp, n_grp), 1)
    rows = jnp.where((rr >> 3) == rl, 1.0, 0.0).astype(BF16)
    tall = jnp.dot(rows, wide, preferred_element_type=F32)
    tr = lax.broadcasted_iota(I32, tall.shape, 0)
    tl = lax.broadcasted_iota(I32, tall.shape, 1)
    lhs = jnp.where((tr & 7) == (tl & 3), tall, 0.0).astype(BF16)
    flat = obs[...].astype(F32).reshape(e_dev * steps, obs.shape[2]).astype(BF16)
    part = jnp.dot(lhs, flat, preferred_element_type=F32)
    encsend[...] = part.reshape(encsend.shape)
    loads[7].wait()
    wall = weights[...].astype(F32)
    shot_row = lax.broadcasted_iota(I32, wall.shape, 0)
    own = jnp.sum(
        jnp.where((group[...] == shot_row) & (shot_row == grp), wall, 0.0),
        axis=0, keepdims=True)
    emit = wall.shape[1]
    ec = ecell[...] - slab * 65536
    ex = jnp.where((ec >= 0) & (ec < 65536), ec >> 8, -1)
    row_e = lax.broadcasted_iota(I32, (256, emit), 0)
    ax = jnp.where(row_e == ex, own, 0.0).astype(BF16)
    ay = jnp.where(row_e == (ec & 255), 1.0, 0.0).astype(BF16)
    amp = lax.dot_general(ax, ay, NT_DOT, preferred_element_type=F32)

    xi = lax.broadcasted_iota(I32, (256, 256), 0)
    yi = lax.broadcasted_iota(I32, (256, 256), 1)

    def up_x(f):
        return jnp.where(xi == 255, 0.0, pltpu.roll(f, 255, 0)) - f

    def up_y(f):
        return jnp.where(yi == 255, 0.0, pltpu.roll(f, 255, 1)) - f

    def down_x(f):
        return f - jnp.where(xi == 0, 0.0, pltpu.roll(f, 1, 0))

    def down_y(f):
        return f - jnp.where(yi == 0, 0.0, pltpu.roll(f, 1, 1))

    has_above = slab < n_slab - 1
    has_below = slab > 0
    for c in loads[8:]:
        c.wait()
    kappa = dens[...] * speed[...] * speed[...]
    keep = 1.0 - atten[...]
    near_out[0] = code((kappa - K_MID) * (TOP / K_MAX))
    near_out[1] = code((keep - D_MID) * (TOP / D_MAX))
    hk = HALF * kappa
    hb = HALF * buoy

    def local_step(p, px, py):
        px = px - hb * up_x(p)
        py = py - hb * up_y(p)
        return px, py, down_x(px) + down_y(py)

    divs = [None] * steps
    recorded = [None] * steps
    p = press[0]
    px, py, flat_div = local_step(p, vel[1], vel[2])
    pz = vel[0] + hb * p
    base = keep * p + wav[0] * amp
    top = 1.001 * (
        top_of(base - hk * (pz + flat_div)) + P_MAX * top_of(hk * hb) + V_MAX * top_of(hk))
    p1_scale[...] = jnp.broadcast_to(top * (1.0 / TOP), (8, 128))
    loads[3].wait()
    pl.semaphore_wait(barrier, n_grp + 5)

    pending = []

    def send(src, dst, to, k):
        c = pltpu.make_async_remote_copy(
            src_ref=src, dst_ref=dst, send_sem=halo_send.at[k], recv_sem=halo_recv.at[k],
            device_id=(to, grp), device_id_type=MESH)
        c.start()
        pending.append(c)
        return c

    cells = [send(rcs.at[3], rcs.at[3 - d], near[d], 27 + d) for d in near]
    p0_down = send(p0_out, p0_in, below, 4)
    w_up = send(w_out, w_in, above, 5)
    b_up = send(near_out.at[2], b_in, above, 6)
    quarter = pl.ds(pl.multiple_of(lax.rem(grp, 4) * 64, 64), 64)
    pieces_in = [
        send(near_out.at[:, quarter], near_in.at[0, :, quarter], below, 0),
        send(near_out.at[0:2, quarter], near_in.at[1, 0:2, quarter], above, 1),
        send(near_out.at[2, quarter], near_in.at[1, 2, quarter], near[2], 33)]

    enc_copies = []
    for d in range(1, n_grp):
        peer = lax.rem(grp + d, n_grp)
        c = pltpu.make_async_remote_copy(
            src_ref=encsend.at[peer], dst_ref=encrecv.at[d], send_sem=enc_send.at[d],
            recv_sem=enc_recv.at[d], device_id=(slab, peer), device_id_type=MESH)
        c.start()
        enc_copies.append(c)
    pending += enc_copies

    for c in cells:
        c.wait_recv()
    row_r = lax.broadcasted_iota(I32, (256, 128), 0)
    col_x, hot_y = {}, {}
    for d in range(-3, 4):
        rc = rcs[d + 3]
        inside = (slab + d >= 0) & (slab + d < n_slab)
        col_x[d] = jnp.where(inside, rc >> 8, -1000)
        y = jnp.where(inside, rc & 255, -1000)
        for dy in (-1, 0, 1) if abs(d) < 3 else (0,):
            hot_y[d, dy] = jnp.where(row_r == y + dy, 1.0, 0.0).astype(BF16)

    star = ((0, -1), (-1, 0), (0, 0), (1, 0), (0, 1))

    def spots(d, others):
        return [(d, dx, dy) for dx, dy in star] + [(o, 0, 0) for o in others]

    def blocks(points):
        return sorted({(d, dy) for d, _, dy in points})

    def gather(pieces, points):
        keys = blocks(points)
        wide = jnp.concatenate([hot_y[key] for key in keys], axis=1)
        values = jnp.dot(
            jnp.concatenate(pieces, axis=1), jnp.concatenate([wide] * len(pieces), axis=0),
            preferred_element_type=F32)
        table = {key: values[:, i * 128:(i + 1) * 128] for i, key in enumerate(keys)}
        return [
            jnp.sum(jnp.where(row_r == col_x[d] + dx, table[d, dy], 0.0), axis=0, keepdims=True)
            for d, dx, dy in points
        ]

    def scatter(values, points, split):
        left = []
        keys = blocks(points)
        for key in keys:
            total = 0.0
            for v, (d, dx, dy) in zip(values, points):
                if (d, dy) == key:
                    total = total + jnp.where(row_r == col_x[d] + dx, v, 0.0)
            left.append(total)
        right = [hot_y[key] for key in keys]
        pieces = [split(x) for x in left]
        count = len(pieces[0])
        lhs = jnp.concatenate([pc[i] for i in range(count) for pc in pieces], axis=1)
        rhs = jnp.concatenate(right * count, axis=1)
        return lax.dot_general(lhs, rhs, NT_DOT, preferred_element_type=F32)

    def column(rows_list):
        pad = 8 - len(rows_list)
        if pad:
            rows_list = rows_list + [jnp.zeros((pad, 128), F32)]
        return jnp.concatenate(rows_list, axis=0)

    only = [(0, 0, 0)]
    ring = spots(0, (1, -1))
    ones = jnp.ones((1, 128), F32)
    plain = lambda v: (v.astype(BF16),)
    count = scatter([ones] * 7, ring, plain)
    inv_ring = jnp.where(count > 0.5, 1.0 / count, 0.0)

    got = [
        send(p1_scale, p1_scale_in.at[0], below, 9), send(p1_scale, p1_scale_in.at[1], above, 10)]
    to_code = TOP / top

    nearby = [(1, 0, 0), (-1, 0, 0)]
    kappa_at = gather(split2(kappa), spots(0, (1, -1)))
    buoy_at = gather(split2(buoy), [(0, 0, 0), (0, -1, 0), (0, 0, -1)] + nearby)
    keep_at = gather(split2(keep), only)[0]
    amp_at = gather(split2(amp), only)[0]

    p0_down.wait_recv()
    w_up.wait_recv()
    b_up.wait_recv()
    b_low = jnp.where(has_below, decode(b_in[...]) * (B_MAX / TOP) + B_MID, 0.0)
    hbl = HALF * b_low
    pzl = jnp.where(has_below, decode(w_in[...]) * (W_MAX / TOP), 0.0) - hbl * p
    pz = pz - hb * jnp.where(has_above, decode(p0_in[...]) * (P_MAX / TOP), 0.0)
    divs[0] = pz - pzl + flat_div
    p = base - hk * divs[0]
    press[1] = p

    p1_out[...] = code(p * to_code)
    got += [send(p1_out, p1_in.at[0], below, 7), send(p1_out, p1_in.at[1], above, 8)]

    low_at = gather(split2(b_low), only + nearby)
    fix_out[...] = column([
        0.25 * kappa_at[5] * buoy_at[3], 0.25 * kappa_at[5] * low_at[1],
        0.25 * kappa_at[6] * buoy_at[4], 0.25 * kappa_at[6] * low_at[2]])
    fixed = [
        send(fix_out, fix_in.at[0], below, 11), send(fix_out, fix_in.at[1], above, 12),
        send(fix_out, fix2_in.at[0], near[-2], 31), send(fix_out, fix2_in.at[1], near[2], 32)]
    for c in pieces_in:
        c.wait_recv()
    planes = []
    for d in range(1, 4):
        c = pltpu.make_async_remote_copy(
            src_ref=near_in.at[:, :, quarter], dst_ref=near_in.at[:, :, quarter],
            send_sem=halo_send.at[(2, 3, 34)[d - 1]], recv_sem=halo_recv.at[(2, 3, 34)[d - 1]],
            device_id=(slab, lax.div(grp, 4) * 4 + lax.rem(lax.rem(grp, 4) + d, 4)),
            device_id_type=MESH)
        c.start()
        planes.append(c)
    pending += planes
    k_at, b_at = kappa_at[2], buoy_at[0]
    own_at = 0.25 * k_at * b_at
    star_at = [
        kappa_at[0] * 0.25 * k_at * buoy_at[2],
        kappa_at[1] * 0.25 * k_at * buoy_at[1],
        k_at * (keep_at - 0.25 * k_at * (3.0 * b_at + buoy_at[1] + buoy_at[2] + low_at[0])),
        kappa_at[3] * own_at,
        kappa_at[4] * own_at]

    recorded[0] = gather(split2(p), only)[0]
    px, py, flat_div = local_step(p, px, py)
    pz = pz + hb * p
    pzl = pzl - hbl * p
    base = keep * p + wav[1] * amp
    for c in got:
        c.wait_recv()
    pz = pz - hb * jnp.where(has_above, decode(p1_in[0]) * p1_scale_in[0, 0:1, 0:1], 0.0)
    pzl = pzl + hbl * (decode(p1_in[1]) * p1_scale_in[1, 0:1, 0:1])
    divs[1] = pz - pzl + flat_div
    p = base - hk * divs[1]
    press[2] = p

    to_up, to_down = spots(1, (0, 2)), spots(-1, (0, -2))
    values = gather(split2(p), to_up + to_down)
    p2_out[0] = column(values[7:])
    p2_out[1] = column(values[:7])
    far_out[0] = column(values[13:])
    far_out[1] = column(values[6:7])
    got = [
        send(p2_out.at[0], p2_in.at[0], below, 13), send(p2_out.at[1], p2_in.at[1], above, 14)]
    far = [
        send(far_out.at[0], far_in.at[0], near[-2], 15),
        send(far_out.at[1], far_in.at[1], near[2], 16)]
    px, py, flat_div = local_step(p, px, py)
    pz = pz + hb * p
    pzl = pzl - hbl * p
    flat_div = pz - pzl + flat_div
    base = keep * p + wav[2] * amp - hk * flat_div
    values = gather(split2(base), nearby)
    part_out[0] = column(values[1:])
    part_out[1] = column(values[:1])
    parts = [
        send(part_out.at[0], part_in.at[0], below, 17),
        send(part_out.at[1], part_in.at[1], above, 18)]
    recorded[1] = gather(split2(p), only)[0]
    for c in got:
        c.wait_recv()
    ua = hb * (inv_ring * scatter(
        [p2_in[0, i:i + 1] for i in range(7)], spots(0, (1, -1)), split2))
    ub = hbl * (inv_ring * scatter(
        [p2_in[1, i:i + 1] for i in range(7)], spots(0, (-1, 1)), split2))
    pz = pz - ua
    pzl = pzl + ub
    divs[2] = flat_div - ua - ub
    p = base + hk * (ua + ub)
    press[3] = p
    recorded[2] = gather(split2(p), only)[0]

    px, py, flat_div = local_step(p, px, py)
    div_at = gather(split2(pz + hb * p - (pzl - hbl * p) + flat_div), only)[0]
    for c in far + fixed + parts:
        c.wait_recv()
    pa = part_in[0, 0:1] + fix_in[0, 2:3] * far_in[0, 0:1] + fix_in[0, 3:4] * recorded[1]
    pb = part_in[1, 0:1] + fix_in[1, 0:1] * recorded[1] + fix_in[1, 1:2] * far_in[1, 0:1]
    pa = jnp.where(has_above, pa, 0.0)
    div_at = div_at - HALF * (b_at * pa + low_at[0] * pb)
    recorded[3] = keep_at * recorded[2] - HALF * k_at * div_at + wav[3] * amp_at

    for c in enc_copies:
        c.wait_recv()
    enc = encsend[grp]
    for d in range(1, n_grp):
        enc = enc + encrecv[d]
    res = [(recorded[t] - enc[t:t + 1]) * (1.0 / n_grp) for t in range(steps)]

    sigma = k_at * res[3]
    star_rows = [v * res[3] for v in star_at]
    star_rows[2] = star_rows[2] + k_at * res[2]
    res_out[...] = column([sigma] + star_rows + [k_at * res[1]])
    got = [
        send(res_out, res_in.at[0], below, 19), send(res_out, res_in.at[1], above, 20),
        send(res_out, res_in.at[2], near[-2], 21), send(res_out, res_in.at[3], near[2], 22),
        send(res_out, res_in.at[4], near[-3], 23), send(res_out, res_in.at[5], near[3], 20 + 15)]

    def spread(b, f):
        return down_x(b * up_x(f)) + down_y(b * up_y(f))

    qb = 0.25 * buoy
    qbl = 0.25 * b_low
    adj = scatter([res[3]], only, split3)
    gd = -adj * press[3]
    gk = scatter([-HALF * res[3] * div_at], only, split3)
    inj = [scatter([res[t]], only, split3) for t in range(steps - 1)]
    total = kappa * adj
    base = inj[2] + keep * adj + spread(qb, total) - (qb + qbl) * total
    for c in planes:
        c.wait_recv()
    k_near = [decode(near_in[i, 0]) * (K_MAX / TOP) + K_MID for i in range(2)]
    d_near = [decode(near_in[i, 1]) * (D_MAX / TOP) + D_MID for i in range(2)]
    k_near[0] = jnp.where(has_above, k_near[0], 0.0)
    b_near = [decode(near_in[i, 2]) * (B_MAX * 0.25 / TOP) + B_MID * 0.25 for i in range(2)]
    b_near[1] = jnp.where(slab > 1, b_near[1], 0.0)
    for c in got:
        c.wait_recv()

    def row(i, k):
        return res_in[i, k:k + 1]

    last, second, outer, first = [], [], [], []
    for i, d in enumerate((1, -1)):
        up, down = (fix_in[i, 0:1], fix_in[i, 3:4])
        up2, down2 = (fix2_in[i, 0:1], fix2_in[i, 3:4])
        out_row, in_row, out2, in2 = (up, down, up2, down2) if d > 0 else (down, up, down2, up2)
        last.append(scatter([row(i, 0)], [(d, 0, 0)], split2))
        first.append(scatter([row(i, 6)], [(d, 0, 0)], split2))
        second.append(scatter(
            [row(i, k) for k in range(1, 6)] + [out_row * row(i + 2, 0), in_row * sigma],
            spots(d, (2 * d, 0)), split2))
        rows_far = [row(i + 2, k) for k in range(1, 6)]
        rows_far[2] = rows_far[2] + row(i + 2, 0)
        outer.append(scatter(
            rows_far + [out2 * row(i + 4, 0), in2 * row(i, 0)],
            spots(2 * d, (3 * d, d)), split2))
    adj = base + qb * last[0] + qbl * last[1]
    gd = gd - adj * press[2]
    gk = gk - HALF * adj * divs[2]
    total = total + kappa * adj
    both = [last[i] + second[i] for i in range(2)]
    sa = first[0] + d_near[0] * second[0] + k_near[0] * (
        spread(b_near[0], both[0]) + b_near[0] * (outer[0] - both[0]) + qb * (total - both[0]))
    sb = first[1] + d_near[1] * second[1] + k_near[1] * (
        spread(qbl, both[1]) + qbl * (total - both[1]) + b_near[1] * (outer[1] - both[1]))
    adj = inj[1] + keep * adj + spread(qb, total) + (
        qb * (both[0] - total) + qbl * (both[1] - total))
    gd = gd - adj * press[1]
    gk = gk - HALF * adj * divs[1]
    total = total + kappa * adj
    adj = inj[0] + keep * adj + spread(qb, total) + (
        qb * (both[0] + sa - total) + qbl * (both[1] + sb - total))
    gd = gd - adj * press[0]
    gk = gk - HALF * adj * divs[0]
    gk = gk * (2.0 * dens[...] * speed[...])
    rows_out = 256 // n_grp
    copies = {d: [] for d in range(1, n_grp)}

    def to_peer(d, src, dst, sends, recvs):
        c = pltpu.make_async_remote_copy(
            src_ref=src, dst_ref=dst, send_sem=sends, recv_sem=recvs,
            device_id=(slab, lax.rem(grp + d, n_grp)), device_id_type=MESH)
        c.start()
        copies[d].append(c)

    for i, g in ((1, gd), (0, gk)):
        grad[i] = g
        top = jnp.maximum(top_of(g), 1e-30)
        coded[i] = code_root(g, top)
        gscale[i] = jnp.broadcast_to(top * (1.0 / (TOP * TOP)), (8, 128))
        for d in range(1, n_grp):
            start = lax.rem(grp + d, n_grp) * rows_out
            to_peer(
                d, coded.at[i, pl.ds(pl.multiple_of(start, rows_out), rows_out)],
                gradrecv.at[d, i], grad_send.at[i, d], grad_recv.at[i, d])
    for d in range(1, n_grp):
        to_peer(d, gscale, gscale_in.at[d], gs_send.at[d], gs_recv.at[d])
    mine = pl.ds(pl.multiple_of(grp * rows_out, rows_out), rows_out)
    total = [grad[0, mine], grad[1, mine]]
    for d in range(1, n_grp):
        for c in copies[d]:
            c.wait_recv()
        for i in range(2):
            total[i] = total[i] + decode_root(gradrecv[d, i]) * gscale_in[d, i, 0:1, 0:1]
    out[0] = total[0]
    out[1] = total[1]
    for c in pending + [c for d in copies for c in copies[d]]:
        c.wait_send()


def shards(
    n_slab, n_grp,
    sound_speed, density, attenuation, wavelet, weights, emitter_group, emitter_cell,
    receiver_cell, pressure_start, velocity_start, observed,
):
    vmem = pl.BlockSpec(memory_space=pltpu.VMEM)
    hbm = pl.BlockSpec(memory_space=pltpu.HBM)
    smem = pl.BlockSpec(memory_space=pltpu.SMEM)
    rows = 256 // n_grp
    plane = lambda *n, t=F32: pltpu.VMEM(n + (256, 256), t)
    tile = lambda *n: pltpu.VMEM(n + (8, 128), F32)
    out = jax.ShapeDtypeStruct((2, rows, 256), F32)
    dma = pltpu.SemaphoreType.DMA
    emit = weights.shape[1]
    both = pl.pallas_call(
        functools.partial(kernel, n_slab, n_grp),
        out_shape=out,
        in_specs=[smem] + [hbm] * 10,
        out_specs=vmem,
        scratch_shapes=[
            plane(), plane(), plane(), plane(4), plane(3),
            pltpu.VMEM(weights.shape, BF16), pltpu.VMEM((1, emit), I32),
            pltpu.VMEM((1, emit), I32), pltpu.VMEM(observed.shape, BF16),
            pltpu.VMEM((7, 1, 128), I32),
            plane(t=I16), plane(t=I16), plane(t=I16),
            plane(t=I16), plane(t=I16), plane(t=I16), plane(2, t=I16),
            tile(), tile(2), tile(2), tile(2), tile(2), tile(2), tile(2), tile(2), tile(), tile(2),
            tile(), tile(6), tile(2), plane(3, t=I16), plane(2, 3, t=I16),
            tile(n_grp), tile(n_grp), plane(2), plane(2, t=I16),
            pltpu.VMEM((n_grp, 2, rows, 256), I16), tile(2), tile(n_grp, 2),
            dma((10,)), dma((36,)), dma((36,)), dma((n_grp,)), dma((n_grp,)),
            dma((2, n_grp)), dma((2, n_grp)), dma((n_grp,)), dma((n_grp,)),
        ],
        compiler_params=pltpu.CompilerParams(
            collective_id=0, has_side_effects=True, vmem_limit_bytes=60 * 1024 * 1024),
    )(
        wavelet, sound_speed, density, attenuation, pressure_start, velocity_start, weights,
        emitter_group.reshape(1, -1), emitter_cell.reshape(1, -1),
        receiver_cell.reshape(1, -1), observed,
    )
    return both[0:1], both[1:2]


def solution(mesh):
    return jax.shard_map(
        functools.partial(shards, mesh.shape["slab"], mesh.shape["grp"]),
        mesh=mesh,
        in_specs=(
            P("slab", None, None),
            P("slab", None, None),
            P("slab", None, None),
            P(),
            P(),
            P(),
            P(),
            P("slab"),
            P("grp", "slab", None, None),
            P(None, "grp", "slab", None, None),
            P("grp", None, "slab"),
        ),
        out_specs=(P("slab", "grp", None), P("slab", "grp", None)),
        check_vma=False,
    )
```
